32 devices in a mesh: ens: 4 (over y, x), grid: 8 (over z, core).
Axes of the slice: x: 2, y: 2, z: 4, core: 2. Of those that a mesh axis runs over, the one named last changes fastest.
Arguments:
- latent: bfloat16 [4, 1024, 2048], P('ens', None, 'grid'), may hold values from -24 to 24
- w_in: bfloat16 [1024, 1024], replicated, may hold values from -0.1875 to 0.1875
- w_out: bfloat16 [99, 1024], replicated, may hold values from -0.1875 to 0.1875
- target: float32 [99, 2048], P(None, 'grid'), may hold values from -6 to 6
- area: float32 [2048], P('grid'), may hold values from 0.05 to 3, as said below
- var_weight: float32 [99], replicated, may hold values from 0.2 to 2
Outputs:
- loss: float32 [], replicated
- grad_latent: bfloat16 [4, 1024, 2048], P('ens', None, 'grid')
- grad_in: float32 [1024, 1024], P('ens', 'grid')
- grad_out: float32 [99, 1024], P(None, 'grid')
The draws below stay inside these ranges and needn't reach their ends.
Inputs may be any that keep to these rules, and one draw needn't show every extreme that they name: Every area weight is positive.
All inputs are finite; a program needn't handle non-finite values.
Results may differ from the reference program's by a relative error of at most 0.013.
Values may be sent and summed in bfloat16 or wider, within the bound.
A program may use at most 64 MiB of HBM per device.

```python
import math
import jax
import jax.numpy as jnp
from jax import lax

LAT = 1024
HID = 1024
VARS = 99
PTS_DEV = 256
MEMBERS = 4
POINTS = 2048
N_GRID = 8


def draw_area(key, part):
    position = jnp.arange(POINTS, dtype=jnp.float32)
    latitude = 1.25 * (1.0 - position / POINTS)
    base = jnp.cos(latitude)
    jitter = jax.random.uniform(key, (POINTS,), jnp.float32, 0.5, 1.5)
    return (base * jitter).astype(jnp.float32)


def draw_latent(key, part):
    value_key = jax.random.fold_in(key, 11)
    pair_key = jax.random.fold_in(key, 23)
    blocks = POINTS // PTS_DEV
    lat_block = LAT // blocks
    pairing = jax.random.permutation(pair_key, blocks)
    point_block = jnp.arange(POINTS, dtype=jnp.int32) // PTS_DEV
    channel_block = jnp.arange(LAT, dtype=jnp.int32) // lat_block
    chosen = pairing[point_block]
    boost = jnp.where(channel_block[:, None] == chosen[None, :], 3.0, 1.0).astype(jnp.float32)
    share = jnp.arange(MEMBERS, dtype=jnp.float32) / float(MEMBERS - 1)
    noise = jax.random.truncated_normal(value_key, -4.0, 4.0, (MEMBERS, LAT, POINTS), jnp.float32)
    member_scale = 0.5 * jnp.exp(share * 1.3862944)
    return (noise * member_scale[:, None, None] * boost[None]).astype(jnp.bfloat16)


def block_levels(stream_key, shape, shards, least, largest):
    loudness = 1.0
    for dim, parts in shards:
        draws = jax.random.uniform(jax.random.fold_in(jax.random.fold_in(stream_key, 6), dim), (parts,), jnp.float32, least / len(shards), largest / len(shards))
        loudness = loudness * jnp.repeat(jnp.exp(draws), shape[dim] // parts).reshape((-1,) + (1,) * (len(shape) - 1 - dim))
    return loudness


def centred(key, shape, scale, bound, shards=(), kind=jnp.bfloat16):
    level = block_levels(key, shape, shards, -0.22, 0.18) if shards else 1.0
    drawn = jax.random.normal(key, shape, jnp.float32) * scale * level
    return jnp.minimum(jnp.maximum(drawn, -bound), bound).astype(kind)


def setup_inputs(seed: int = 0) -> dict:
    splits = jax.random.split(jax.random.key(seed), 7)
    latent = draw_latent(jax.random.fold_in(splits[6], 71), 0)
    w_in = centred(splits[1], (HID, LAT), LAT ** -0.5, 0.1875)
    w_out = centred(splits[2], (VARS, HID), HID ** -0.5, 0.1875)
    target = centred(splits[3], (VARS, POINTS), 1.0, 6.0, ((1, 8),), jnp.float32)
    area = draw_area(jax.random.fold_in(splits[6], 71), 0)
    var_weight = jnp.clip(jnp.exp(jax.random.uniform(splits[5], (VARS,), jnp.float32, math.log(0.2), math.log(2.0))), 0.2, 2.0)
    return {"latent": latent, "w_in": w_in, "w_out": w_out, "target": target, "area": area, "var_weight": var_weight}


smooth_sq = 0.01
gelu_c = 0.7978845608
gelu_k = 0.044715

def gelu_value(value):
    inner = jnp.tanh(gelu_c * (value + gelu_k * value * value * value))
    return 0.5 * value * (1.0 + inner)

def gelu_slope(value):
    inner = jnp.tanh(gelu_c * (value + gelu_k * value * value * value))
    return 0.5 * (1.0 + inner) + 0.5 * value * (1.0 - inner * inner) * gelu_c * (1.0 + 3.0 * gelu_k * value * value)

def distance(value):
    return jnp.sqrt(value * value + smooth_sq)

def distance_slope(value):
    return value / jnp.sqrt(value * value + smooth_sq)

def reference(latent, w_in, w_out, target, area, var_weight):
    count = float(MEMBERS)

    def forward(features):
        preact = jnp.dot(w_in, features, preferred_element_type=jnp.float32)
        hidden = gelu_value(preact).astype(jnp.bfloat16)
        decoded = jnp.dot(w_out, hidden, preferred_element_type=jnp.float32)
        return (preact, hidden, decoded)
    decoded_all = lax.map(lambda features: forward(features)[2], latent)

    def pairs(own):
        spread = own[None] - decoded_all
        return (lax.optimization_barrier(jnp.sum(distance(spread), 0)), lax.optimization_barrier(jnp.sum(distance_slope(spread), 0)))
    pair_sum, pair_slope = lax.map(pairs, decoded_all)
    weight_total = jnp.sum(area)
    weight = area[None, :] * var_weight[:, None]
    skill = distance(decoded_all - target[None])
    local = skill / count - pair_sum / (2.0 * count * (count - 1.0))
    loss = jnp.sum(weight[None] * local) / (weight_total * VARS)
    factor = POINTS / (weight_total * VARS)

    def member_step(carry, inputs):
        features, decoded, slope_pairs = inputs
        preact, hidden, unused = forward(features)
        dout = (factor * weight * (distance_slope(decoded - target) / count - slope_pairs / (count * (count - 1.0)))).astype(jnp.bfloat16)
        dhidden = lax.dot_general(w_out, dout, (((0,), (0,)), ((), ())), preferred_element_type=jnp.float32)
        dpre = (dhidden * gelu_slope(preact)).astype(jnp.bfloat16)
        grad_lat = lax.dot_general(w_in, dpre, (((0,), (0,)), ((), ())), preferred_element_type=jnp.float32).astype(jnp.bfloat16)
        dpre_blocks = dpre.reshape(HID, N_GRID, PTS_DEV).astype(jnp.float32)
        feat_blocks = features.reshape(LAT, N_GRID, PTS_DEV).astype(jnp.float32)
        term_in = jnp.einsum('hcp,lcp->chl', dpre_blocks, feat_blocks).astype(jnp.bfloat16).astype(jnp.float32)
        dout_blocks = dout.reshape(VARS, N_GRID, PTS_DEV).astype(jnp.float32)
        hid_blocks = hidden.reshape(HID, N_GRID, PTS_DEV).astype(jnp.float32)
        term_out = jnp.einsum('vcp,hcp->cvh', dout_blocks, hid_blocks).astype(jnp.bfloat16).astype(jnp.float32)
        total_in, total_out = carry
        return ((total_in + lax.optimization_barrier(jnp.sum(term_in, 0)), total_out + lax.optimization_barrier(jnp.sum(term_out, 0))), grad_lat)
    start = (jnp.zeros((HID, LAT), jnp.float32), jnp.zeros((VARS, HID), jnp.float32))
    (total_in, total_out), grad_latent = lax.scan(member_step, start, (latent, decoded_all, pair_slope))
    ratio = 1.0 / jnp.sqrt(jnp.float32(POINTS) * jnp.float32(MEMBERS))
    return (loss, grad_latent, ratio * total_in, ratio * total_out)
```

```python
import functools

import jax
import jax.numpy as jnp
import numpy as np
from jax import lax
from jax.experimental import pallas as pl
from jax.experimental.pallas import tpu as pltpu
from jax.sharding import PartitionSpec as P

SMOOTH = 0.01
GELU_C = 0.7978845608
GELU_K = 0.044715
F32 = jnp.float32
BF16 = jnp.bfloat16


def dot_nn(a, b):
    return jnp.dot(a, b, preferred_element_type=F32)


def dot_nt(a, b):
    return lax.dot_general(a, b, (((1,), (1,)), ((), ())), preferred_element_type=F32)


def dot_tn(a, b):
    return lax.dot_general(a, b, (((0,), (0,)), ((), ())), preferred_element_type=F32)


class Sizes:
    def __init__(self, n, ng, hid, lat, nvars, pts):
        self.n, self.ng, self.hid, self.lat, self.nvars, self.pts = n, ng, hid, lat, nvars, pts
        self.nz = ng // 2
        self.nb = n.bit_length() - 1
        self.cols = lat // ng
        self.rows_e = hid // n
        self.half = self.rows_e // 2
        self.vrow = -(-(-(-nvars // n)) // 16) * 16
        self.vpad = self.vrow * n
        self.tile = max(256, 2 * self.cols)
        self.tiles = hid // self.tile
        self.copies = 3 * ng + 4 * n + 8 + self.tiles + (2 * self.nz + 1) * (self.nb + 1) + 2 * self.nz + n


def stage_index(nb, order, stage, value):
    index = [slice(None)] * nb
    for bit in order[:stage]:
        index[nb - 1 - bit] = 0
    index[nb - 1 - order[stage]] = value
    return tuple(index)


def kernel(
    s,
    lat_hbm, win_hbm, wout_ref, target_ref, area_ref, vw_ref,
    loss_ref, glat_hbm, gin_ref, gout_ref,
    lat_s, latp, win_s, wo32, wo_s, wot, hid_s, hidp, slope_s, dec_s, dec_in, tgt_s, vrow_s, vcol_s, area_all,
    dout_o, dout_s, doutp, loss_e, loss_g, dpre_s, dprep, glat_s, gall,
    acc, snd, acc_o, snd_o, tmp_o, zsnd, zrcv, zsnd_o, zrcv_o, *rest,
):
    nb, n, ng, nz = s.nb, s.n, s.ng, s.nz
    rcv, rcv_o = rest[:nb], rest[nb:2 * nb]
    send_sem, recv_sem, local_sem = rest[2 * nb:]
    me = lax.axis_index("ens")
    g = lax.axis_index("grid")
    core = g % 2
    chip = g // 2
    bits = [(me // (1 << i)) % 2 for i in range(nb)]
    used = [0]

    def ens_peer(r):
        return sum((bits[i] + ((r >> i) & 1) * (1 - 2 * bits[i])) * (1 << i) for i in range(nb))

    def remote(src, dst, device):
        i = used[0]
        used[0] += 1
        copy = pltpu.make_async_remote_copy(
            src_ref=src, dst_ref=dst, send_sem=send_sem.at[i], recv_sem=recv_sem.at[i],
            device_id=device, device_id_type=pl.DeviceIdType.MESH,
        )
        copy.start()
        sent.append(copy)
        return copy

    sent = []
    twin = {"grid": g + 1 - 2 * core}
    ens_peers = [None] + [{"ens": ens_peer(r)} for r in range(1, n)]
    grid_peers = [None] + [{"grid": (g + o) % ng} for o in range(1, ng)]

    get_lat = pltpu.make_async_copy(lat_hbm, lat_s, local_sem.at[0])
    get_win = pltpu.make_async_copy(win_hbm, win_s, local_sem.at[1])
    get_lat.start()
    get_win.start()
    barrier = pltpu.get_barrier_semaphore()
    for peer in ens_peers[1:] + grid_peers[1:]:
        pl.semaphore_signal(barrier, inc=1, device_id=peer, device_id_type=pl.DeviceIdType.MESH)

    arow = area_ref[...].reshape(1, s.pts)
    area_all[0] = jnp.broadcast_to(arow, (8, s.pts))
    wo32[...] = jnp.zeros_like(wo32)
    wo32[0:s.nvars, :] = wout_ref[...].astype(F32)
    wo_s[...] = wo32[...].astype(BF16)
    tgt_s[...] = jnp.zeros_like(tgt_s)
    tgt_s[0:s.nvars, :] = target_ref[...]
    vrow_s[...] = jnp.zeros_like(vrow_s)
    vrow_s[0:1, 0:s.nvars] = vw_ref[...].reshape(1, s.nvars)

    pl.semaphore_wait(barrier, n + ng - 2)
    lat_copy = remote(lat_hbm.at[:, 1 - core], latp, twin)
    area_copies = [remote(area_all.at[0], area_all.at[o], grid_peers[o]) for o in range(1, ng)]

    get_lat.wait()
    get_win.wait()
    span = s.tile // (2 * s.cols)

    def forward(i, carry):
        rows = pl.ds(pl.multiple_of(i * s.tile, s.tile), s.tile)
        v = dot_nn(win_s[rows, :], lat_s[...].reshape(s.lat, s.pts))
        t = jnp.tanh(GELU_C * (v + GELU_K * v * v * v))
        hid_s[pl.ds(i * span, span)] = (0.5 * v * (1.0 + t)).astype(BF16).reshape(span, 2, s.cols, s.pts)
        slope_s[rows, :] = 0.5 * (1.0 + t) + 0.5 * v * (1.0 - t * t) * GELU_C * (1.0 + 3.0 * GELU_K * v * v)
        return carry

    lax.fori_loop(0, s.tiles, forward, 0)
    dec_s[...] = dot_nn(wo_s[...], hid_s[...].reshape(s.hid, s.pts)).reshape(n, s.vrow, s.pts)

    dec_copies = [remote(dec_s.at[ens_peer(r)], dec_in.at[r], ens_peers[r]) for r in range(1, n)]
    hid_copy = remote(hid_s.at[:, 1 - core], hidp, twin)
    dec_in[0] = dec_s[me]
    wot[...] = wo32[...].T.astype(BF16)
    square = (s.vpad, s.vpad)
    eye = lax.broadcasted_iota(jnp.int32, square, 0) == lax.broadcasted_iota(jnp.int32, square, 1)
    column = jnp.sum(jnp.where(eye, jnp.broadcast_to(vrow_s[0:1, :], square), 0.0), axis=1, keepdims=True)
    vcol_s[...] = jnp.broadcast_to(column, vcol_s.shape)
    mine = pl.ds(pl.multiple_of(me * s.vrow, s.vrow), s.vrow)
    weight = vcol_s[mine, 0:1] * arow
    target = tgt_s[mine, :]
    for copy in area_copies:
        copy.wait_recv()
    total = jnp.sum(area_all[...][:, 0, :].reshape(ng, s.pts), axis=1, keepdims=True)
    total = jnp.sum(total, axis=0, keepdims=True)
    scale = 1.0 / (total * float(s.nvars))
    wide = (float(ng * s.pts) * scale) * weight
    for copy in dec_copies:
        copy.wait_recv()
    members = [dec_in[r] for r in range(n)]
    slopes = [None] * n
    pairs = jnp.full((s.vrow, s.pts), float(n) * float(np.sqrt(np.float32(SMOOTH))), F32)
    for m in range(n):
        for k in range(m):
            u = members[m] - members[k]
            q = u * u + SMOOTH
            root = lax.rsqrt(q)
            pairs = pairs + 2.0 * (q * root)
            slope = u * root
            slopes[m] = slope if slopes[m] is None else slopes[m] + slope
            slopes[k] = -slope if slopes[k] is None else slopes[k] - slope
    local = pairs * (-1.0 / (2.0 * n * (n - 1.0)))
    dout_copies = []
    for r in range(n - 1, -1, -1):
        u = members[r] - target
        q = u * u + SMOOTH
        root = lax.rsqrt(q)
        local = local + (q * root) * (1.0 / n)
        d = (wide * (u * root * (1.0 / n) - slopes[r] * (1.0 / (n * (n - 1.0))))).astype(BF16)
        if r:
            dout_o[r] = d
            dout_copies.append(remote(dout_o.at[r], dout_s.at[me], ens_peers[r]))
        else:
            dout_s[me] = d
    part = jnp.sum(jnp.sum(weight * local, axis=1, keepdims=True), axis=0, keepdims=True)
    loss_e[0] = jnp.broadcast_to(part, (8, 128))
    loss_copies = [remote(loss_e.at[0], loss_e.at[r], ens_peers[r]) for r in range(1, n)]

    for copy in dout_copies:
        copy.wait_recv()
    dout_copy = remote(dout_s, doutp, twin)
    dout = dout_s[...].reshape(s.vpad, s.pts)
    dpre_copies = []
    for i in range(s.tiles):
        rows = pl.ds(i * s.tile, s.tile)
        dpre_s[rows, :] = (dot_nn(wot[rows, :], dout) * slope_s[rows, :]).astype(BF16)
        dpre_copies.append(remote(dpre_s.at[rows], dprep.at[rows], twin))

    def chip_at(k):
        return (chip + nz - 1 - k) % nz

    up, down = list(range(nb)), list(range(nb))[::-1]

    def relative(r):
        return tuple((r >> (nb - 1 - axis)) & 1 for axis in range(nb))

    def start(sums, send, into, order, stage):
        index = stage_index(nb, order, stage, 1)
        send[index] = sums[index].astype(BF16)
        bit = order[stage]
        return remote(send.at[index], into, ens_peers[1 << bit])

    def absorb(copy, sums, into, order, stage):
        copy.wait_recv()
        index = stage_index(nb, order, stage, 0)
        sums[index] = sums[index] + into[...].astype(F32)

    for copy in loss_copies:
        copy.wait_recv()
    here = loss_e[0]
    for r in range(1, n):
        here = here + loss_e[r]
    loss_g[0] = here
    loss_copies = [remote(loss_g.at[0], loss_g.at[o], grid_peers[o]) for o in range(1, ng)]

    hid_copy.wait_recv()
    dout_copy.wait_recv()
    for k in range(nz):
        z = chip_at(k)
        term = dot_nt(dout, hid_s[z, core]) + dot_nt(doutp[...].reshape(s.vpad, s.pts), hidp[z])
        tmp_o[...] = term.reshape(n, s.vrow, s.cols)
        for r in range(n):
            acc_o[relative(r) + (k,)] = tmp_o[ens_peer(r)]
    out_copy = start(acc_o, snd_o, rcv_o[0], up, 0)

    lat_copy.wait_recv()
    for copy in dpre_copies:
        copy.wait_recv()
    moves = []
    for k in range(nz):
        z = chip_at(k)
        own, other = lat_s[z, core], latp[z]
        for r in range(n):
            rows = pl.ds(pl.multiple_of(ens_peer(r) * s.rows_e, s.rows_e), s.rows_e)
            term = dot_nt(dpre_s[rows, :], own) + dot_nt(dprep[rows, :], other)
            acc[(k, 0) + relative(r)] = term[:s.half]
            acc[(k, 1) + relative(r)] = term[s.half:]
        moves.append([
            start(acc.at[k, h], snd.at[k, h], rcv[0].at[k, h], order, 0)
            for h, order in enumerate((up, down))
        ])

    width = s.lat // 4
    puts = []

    def latent_part(j):
        at = pl.ds(j * width, width)
        glat_s[at, :] = dot_tn(win_s[:, at], dpre_s[...]).astype(BF16)
        put = pltpu.make_async_copy(glat_s.at[at], glat_hbm.at[0, at], local_sem.at[2 + j])
        put.start()
        puts.append(put)

    latent_part(0)
    zero = (0,) * nb
    for stage in range(nb):
        absorb(out_copy, acc_o, rcv_o[stage], up, stage)
        if stage < nb - 1:
            out_copy = start(acc_o, snd_o, rcv_o[stage + 1], up, stage + 1)
        for k in range(nz):
            for h, order in enumerate((up, down)):
                absorb(moves[k][h], acc.at[k, h], rcv[stage].at[k, h], order, stage)
                if stage < nb - 1:
                    moves[k][h] = start(acc.at[k, h], snd.at[k, h], rcv[stage + 1].at[k, h], order, stage + 1)
            if stage == nb - 1 and k < nz - 1:
                zsnd[k] = acc[(k, slice(None)) + zero].astype(BF16)
                peer = {"grid": chip_at(k) * 2 + core}
                moves[k] = remote(zsnd.at[k], zrcv.at[k], peer)
        if stage == nb - 1:
            out_moves = []
            for k in range(nz - 1):
                zsnd_o[k] = acc_o[zero + (k,)].astype(BF16)
                peer = {"grid": chip_at(k) * 2 + core}
                out_moves.append(remote(zsnd_o.at[k], zrcv_o.at[k], peer))
        if stage == 0:
            latent_part(1)
            latent_part(2)
            latent_part(3)

    ratio = float(1.0 / np.sqrt(np.float32(ng * s.pts) * np.float32(n)))
    block = acc_o[zero + (nz - 1,)]
    for k in range(nz - 1):
        out_moves[k].wait_recv()
        block = block + zrcv_o[k].astype(F32)
    gall[mine, :] = ratio * block
    gathers = [remote(gall.at[mine], gall.at[mine], ens_peers[r]) for r in range(1, n)]
    block = acc[(nz - 1, slice(None)) + zero]
    for k in range(nz - 1):
        moves[k].wait_recv()
        block = block + zrcv[k].astype(F32)
    gin_ref[...] = (ratio * block).reshape(s.rows_e, s.cols)
    for copy in loss_copies:
        copy.wait_recv()
    loss = loss_g[0]
    for o in range(1, ng):
        loss = loss + loss_g[o]
    loss_ref[...] = loss[0:1, 0:1] * scale
    for copy in gathers:
        copy.wait_recv()
    gout_ref[...] = gall[0:s.nvars, :]
    for copy in sent:
        copy.wait_send()
    for put in puts:
        put.wait()


def per_device(n, ng, latent, w_in, w_out, target, area, var_weight):
    hid, lat = w_in.shape
    pts = latent.shape[2]
    nvars = w_out.shape[0]
    s = Sizes(n, ng, hid, lat, nvars, pts)
    nz, nb, cols = s.nz, s.nb, s.cols
    cube = (2,) * nb
    vmem = pl.BlockSpec(memory_space=pltpu.VMEM)
    anywhere = pl.BlockSpec(memory_space=pl.ANY)
    scratch = [
        pltpu.VMEM((nz, 2, cols, pts), BF16),
        pltpu.VMEM((nz, cols, pts), BF16),
        pltpu.VMEM((hid, lat), BF16),
        pltpu.VMEM((s.vpad, hid), F32),
        pltpu.VMEM((s.vpad, hid), BF16),
        pltpu.VMEM((hid, s.vpad), BF16),
        pltpu.VMEM((nz, 2, cols, pts), BF16),
        pltpu.VMEM((nz, cols, pts), BF16),
        pltpu.VMEM((hid, pts), F32),
        pltpu.VMEM((n, s.vrow, pts), F32),
        pltpu.VMEM((n, s.vrow, pts), F32),
        pltpu.VMEM((s.vpad, pts), F32),
        pltpu.VMEM((8, s.vpad), F32),
        pltpu.VMEM((s.vpad, 128), F32),
        pltpu.VMEM((ng, 8, pts), F32),
        pltpu.VMEM((n, s.vrow, pts), BF16),
        pltpu.VMEM((n, s.vrow, pts), BF16),
        pltpu.VMEM((n, s.vrow, pts), BF16),
        pltpu.VMEM((n, 8, 128), F32),
        pltpu.VMEM((ng, 8, 128), F32),
        pltpu.VMEM((hid, pts), BF16),
        pltpu.VMEM((hid, pts), BF16),
        pltpu.VMEM((lat, pts), BF16),
        pltpu.VMEM((s.vpad, cols), F32),
        pltpu.VMEM((nz, 2) + cube + (s.half, cols), F32),
        pltpu.VMEM((nz, 2) + cube + (s.half, cols), BF16),
        pltpu.VMEM(cube + (nz, s.vrow, cols), F32),
        pltpu.VMEM(cube + (nz, s.vrow, cols), BF16),
        pltpu.VMEM((n, s.vrow, cols), F32),
        pltpu.VMEM((nz - 1, 2, s.half, cols), BF16),
        pltpu.VMEM((nz - 1, 2, s.half, cols), BF16),
        pltpu.VMEM((nz - 1, s.vrow, cols), BF16),
        pltpu.VMEM((nz - 1, s.vrow, cols), BF16),
    ]
    scratch += [pltpu.VMEM((nz, 2) + cube[1 + i:] + (s.half, cols), BF16) for i in range(nb)]
    scratch += [pltpu.VMEM(cube[1 + i:] + (nz, s.vrow, cols), BF16) for i in range(nb)]
    scratch += [
        pltpu.SemaphoreType.DMA((s.copies,)),
        pltpu.SemaphoreType.DMA((s.copies,)),
        pltpu.SemaphoreType.DMA((6,)),
    ]
    loss, grad_lat, grad_in, grad_out = pl.pallas_call(
        functools.partial(kernel, s),
        out_shape=(
            jax.ShapeDtypeStruct((1, 1), F32),
            jax.ShapeDtypeStruct((1, lat, pts), BF16),
            jax.ShapeDtypeStruct((s.rows_e, cols), F32),
            jax.ShapeDtypeStruct((nvars, cols), F32),
        ),
        in_specs=[anywhere, anywhere, vmem, vmem, vmem, vmem],
        out_specs=(vmem, anywhere, vmem, vmem),
        scratch_shapes=scratch,
        compiler_params=pltpu.CompilerParams(
            collective_id=0, has_side_effects=True, vmem_limit_bytes=48 * 1024 * 1024
        ),
        name="crps_backward",
    )(latent.reshape(nz, 2, cols, pts), w_in, w_out, target, area, var_weight)
    return loss[0, 0], grad_lat, grad_in, grad_out


def solution(mesh):
    in_specs = (P("ens", None, "grid"), P(), P(), P(None, "grid"), P("grid"), P())
    out_specs = (P(), P("ens", None, "grid"), P("ens", "grid"), P(None, "grid"))
    body = functools.partial(per_device, mesh.shape["ens"], mesh.shape["grid"])
    return jax.shard_map(
        body, mesh=mesh, in_specs=in_specs, out_specs=out_specs, check_vma=False
    )
```

```python
import functools

import jax
import jax.numpy as jnp
import numpy as np
from jax import lax
from jax.experimental import pallas as pl
from jax.experimental.pallas import tpu as pltpu
from jax.sharding import PartitionSpec as P

SMOOTH = 0.01
GELU_C = 0.7978845608
GELU_K = 0.044715
F32 = jnp.float32
BF16 = jnp.bfloat16
VMEM_BYTES = 62 * 1024 * 1024


def dot_nn(a, b):
    return jnp.dot(a, b, preferred_element_type=F32)


def dot_nt(a, b):
    return lax.dot_general(a, b, (((1,), (1,)), ((), ())), preferred_element_type=F32)


def dot_tn(a, b):
    return lax.dot_general(a, b, (((0,), (0,)), ((), ())), preferred_element_type=F32)


class Sizes:
    def __init__(self, n, ng, hid, lat, nvars, pts):
        self.n, self.ng, self.hid, self.lat, self.nvars, self.pts = n, ng, hid, lat, nvars, pts
        self.nz = ng // 2
        self.nb = n.bit_length() - 1
        self.cols = lat // ng
        self.rows_e = hid // n
        self.half = self.rows_e // 2
        self.vrow = -(-(-(-nvars // n)) // 16) * 16
        self.vpad = self.vrow * n
        self.tile = max(256, 2 * self.cols)
        self.tiles = hid // self.tile
        self.copies = 3 * ng + 4 * n + 8 + self.tiles + (2 * self.nz + 1) * (self.nb + 1) + 2 * self.nz + n


def stage_index(nb, order, stage, value):
    index = [slice(None)] * nb
    for bit in order[:stage]:
        index[nb - 1 - bit] = 0
    index[nb - 1 - order[stage]] = value
    return tuple(index)


def kernel(
    s,
    lat_hbm, win_hbm, wout_hbm, target_hbm, area_ref, vw_ref,
    loss_ref, glat_hbm, gin_ref, gout_ref,
    lat_s, latp, win_s, wint, wout_ref, target_ref, wo32, wo_s, wot, hid_s, hidp, slope_s, dec_s, dec_in, tgt_s, vrow_s, vcol_s, area_all,
    dout_o, dout_s, doutp, loss_e, loss_g, dpre_s, dprep, glat_s, gall,
    tmp, acc, snd, acc_o, snd_o, tmp_o, zsnd, zrcv, zsnd_o, zrcv_o, *rest,
):
    nb, n, ng, nz = s.nb, s.n, s.ng, s.nz
    rcv, rcv_o = rest[:nb], rest[nb:2 * nb]
    send_sem, recv_sem, local_sem = rest[2 * nb:]
    me = lax.axis_index("ens")
    g = lax.axis_index("grid")
    core = g % 2
    chip = g // 2
    bits = [(me // (1 << i)) % 2 for i in range(nb)]
    used = [0]

    def ens_peer(r):
        return sum((bits[i] + ((r >> i) & 1) * (1 - 2 * bits[i])) * (1 << i) for i in range(nb))

    def remote(src, dst, device):
        i = used[0]
        used[0] += 1
        copy = pltpu.make_async_remote_copy(
            src_ref=src, dst_ref=dst, send_sem=send_sem.at[i], recv_sem=recv_sem.at[i],
            device_id=device, device_id_type=pl.DeviceIdType.MESH,
        )
        copy.start()
        sent.append(copy)
        return copy

    sent = []
    twin = {"grid": g + 1 - 2 * core}
    ens_peers = [None] + [{"ens": ens_peer(r)} for r in range(1, n)]
    grid_peers = [None] + [{"grid": (g + o) % ng} for o in range(1, ng)]

    def win_tile(i):
        rows = pl.ds(pl.multiple_of(i * s.tile, s.tile), s.tile)
        return pltpu.make_async_copy(win_hbm.at[rows], win_s.at[rows], local_sem.at[3 + i])

    get_lat = pltpu.make_async_copy(lat_hbm, lat_s, local_sem.at[0])
    get_out = pltpu.make_async_copy(wout_hbm, wout_ref, local_sem.at[1])
    get_target = pltpu.make_async_copy(target_hbm, target_ref, local_sem.at[2])
    get_lat.start()
    for i in range(s.tiles):
        win_tile(i).start()
    get_out.start()
    get_target.start()
    barrier = pltpu.get_barrier_semaphore()
    for peer in ens_peers[1:] + grid_peers[1:]:
        pl.semaphore_signal(barrier, inc=1, device_id=peer, device_id_type=pl.DeviceIdType.MESH)

    arow = area_ref[...].reshape(1, s.pts)
    area_all[0] = jnp.broadcast_to(jnp.sum(arow, axis=1, keepdims=True), (8, 128))
    vrow_s[...] = jnp.zeros_like(vrow_s)
    vrow_s[0:1, 0:s.nvars] = vw_ref[...].reshape(1, s.nvars)
    wo32[...] = jnp.zeros_like(wo32)
    tgt_s[...] = jnp.zeros_like(tgt_s)

    get_lat.wait()
    span = s.tile // (2 * s.cols)

    def forward(i, carry):
        rows = pl.ds(pl.multiple_of(i * s.tile, s.tile), s.tile)
        win_tile(i).wait()
        v = dot_nn(win_s[rows, :], lat_s[...].reshape(s.lat, s.pts))
        t = jnp.tanh(GELU_C * (v + GELU_K * v * v * v))
        hid_s[pl.ds(i * span, span)] = (0.5 * v * (1.0 + t)).astype(BF16).reshape(span, 2, s.cols, s.pts)
        slope_s[rows, :] = 0.5 * (1.0 + t) + 0.5 * v * (1.0 - t * t) * GELU_C * (1.0 + 3.0 * GELU_K * v * v)
        return carry

    lax.fori_loop(0, s.tiles, forward, 0)
    get_out.wait()
    wo32[0:s.nvars, :] = wout_ref[...].astype(F32)
    wo_s[...] = wo32[...].astype(BF16)
    dec_s[...] = dot_nn(wo_s[...], hid_s[...].reshape(s.hid, s.pts)).reshape(n, s.vrow, s.pts)
    pl.semaphore_wait(barrier, n + ng - 2)

    dec_copies = [remote(dec_s.at[ens_peer(r)], dec_in.at[r], ens_peers[r]) for r in range(1, n)]
    area_copies = [remote(area_all.at[0], area_all.at[o], grid_peers[o]) for o in range(1, ng)]
    hid_copy = remote(hid_s.at[:, 1 - core], hidp, twin)
    lat_copy = remote(lat_hbm.at[:, 1 - core], latp, twin)
    dec_in[0] = dec_s[me]
    get_target.wait()
    tgt_s[0:s.nvars, :] = target_ref[...]
    wot[...] = wo32[...].T.astype(BF16)
    square = (s.vpad, s.vpad)
    eye = lax.broadcasted_iota(jnp.int32, square, 0) == lax.broadcasted_iota(jnp.int32, square, 1)
    column = jnp.sum(jnp.where(eye, jnp.broadcast_to(vrow_s[0:1, :], square), 0.0), axis=1, keepdims=True)
    vcol_s[...] = jnp.broadcast_to(column, vcol_s.shape)
    mine = pl.ds(pl.multiple_of(me * s.vrow, s.vrow), s.vrow)
    weight = vcol_s[mine, 0:1] * arow
    target = tgt_s[mine, :]
    turned = s.lat // 4

    def turn(j):
        at = pl.ds(j * turned, turned)
        wint[at, :] = win_s[:, at].T

    turn(0)
    turn(1)
    for copy in area_copies:
        copy.wait_recv()
    total = area_all[0]
    for o in range(1, ng):
        total = total + area_all[o]
    total = total[0:1, 0:1]
    scale = 1.0 / (total * float(s.nvars))
    wide = (float(ng * s.pts) * scale) * weight
    for copy in dec_copies:
        copy.wait_recv()
    members = [dec_in[r] for r in range(n)]
    slopes = [None] * n
    pairs = jnp.full((s.vrow, s.pts), float(n) * float(np.sqrt(np.float32(SMOOTH))), F32)
    for m in range(n):
        for k in range(m):
            u = members[m] - members[k]
            q = u * u + SMOOTH
            root = lax.rsqrt(q)
            pairs = pairs + 2.0 * (q * root)
            slope = u * root
            slopes[m] = slope if slopes[m] is None else slopes[m] + slope
            slopes[k] = -slope if slopes[k] is None else slopes[k] - slope
    local = pairs * (-1.0 / (2.0 * n * (n - 1.0)))
    dout_copies = []
    for r in range(n - 1, -1, -1):
        u = members[r] - target
        q = u * u + SMOOTH
        root = lax.rsqrt(q)
        local = local + (q * root) * (1.0 / n)
        d = (wide * (u * root * (1.0 / n) - slopes[r] * (1.0 / (n * (n - 1.0))))).astype(BF16)
        if r:
            dout_o[r] = d
            dout_copies.append(remote(dout_o.at[r], dout_s.at[me], ens_peers[r]))
        else:
            dout_s[me] = d
    part = jnp.sum(jnp.sum(weight * local, axis=1, keepdims=True), axis=0, keepdims=True)
    loss_e[0] = jnp.broadcast_to(part, (8, 128))
    loss_copies = [remote(loss_e.at[0], loss_e.at[r], ens_peers[r]) for r in range(1, n)]

    turn(2)
    turn(3)
    for copy in dout_copies:
        copy.wait_recv()
    dout_copy = remote(dout_s, doutp, twin)
    dout = dout_s[...].reshape(s.vpad, s.pts)
    dpre_copies = []
    for i in range(s.tiles):
        rows = pl.ds(i * s.tile, s.tile)
        dpre_s[rows, :] = (dot_nn(wot[rows, :], dout) * slope_s[rows, :]).astype(BF16)
        dpre_copies.append(remote(dpre_s.at[rows], dprep.at[rows], twin))

    def chip_at(k):
        return (chip + nz - 1 - k) % nz

    up, down = list(range(nb)), list(range(nb))[::-1]

    def relative(r):
        return tuple((r >> (nb - 1 - axis)) & 1 for axis in range(nb))

    def place(value, sums, send, at, r, order):
        if (r >> order[0]) & 1:
            send[at] = value.astype(BF16)
        else:
            sums[at] = value

    def start(sums, send, into, order, stage):
        index = stage_index(nb, order, stage, 1)
        if stage:
            send[index] = sums[index].astype(BF16)
        return remote(send.at[index], into, ens_peers[1 << order[stage]])

    def absorb(copy, sums, into, order, stage):
        copy.wait_recv()
        index = stage_index(nb, order, stage, 0)
        sums[index] = sums[index] + into[...].astype(F32)

    for copy in loss_copies:
        copy.wait_recv()
    here = loss_e[0]
    for r in range(1, n):
        here = here + loss_e[r]
    loss_g[0] = here
    loss_copies = [remote(loss_g.at[0], loss_g.at[o], grid_peers[o]) for o in range(1, ng)]

    hid_copy.wait_recv()
    dout_copy.wait_recv()
    group = max(1, min(nz, 256 // s.cols))
    wide_rows = (group * s.cols, s.pts)
    doutp_all = doutp[...].reshape(s.vpad, s.pts)
    for first in range(0, nz, group):
        zs = [chip_at(k) for k in range(first, first + group)]
        own = jnp.stack([hid_s[z, core] for z in zs]).reshape(wide_rows)
        other = jnp.stack([hidp[z] for z in zs]).reshape(wide_rows)
        tmp_o[...] = (dot_nt(dout, own) + dot_nt(doutp_all, other)).reshape(n, s.vrow, group * s.cols)
        for r in range(n):
            for k in range(group):
                value = tmp_o[ens_peer(r), :, k * s.cols:(k + 1) * s.cols]
                place(value, acc_o, snd_o, relative(r) + (first + k,), r, up)
    out_copy = start(acc_o, snd_o, rcv_o[0], up, 0)

    moves = [None] * nz
    orders = (up, down)
    lat_copy.wait_recv()
    for first in range(0, nz, group):
        zs = [chip_at(k) for k in range(first, first + group)]
        own = jnp.stack([lat_s[z, core] for z in zs]).reshape(wide_rows)
        other = jnp.stack([latp[z] for z in zs]).reshape(wide_rows)
        for i in range(s.tiles):
            rows = pl.ds(i * s.tile, s.tile)
            tmp[rows, :] = dot_nt(dpre_s[rows, :], own)
        for i in range(s.tiles):
            if first == 0:
                dpre_copies[i].wait_recv()
            rows = pl.ds(i * s.tile, s.tile)
            tmp[rows, :] += dot_nt(dprep[rows, :], other)
        for k in range(first, first + group):
            lanes = slice((k - first) * s.cols, (k - first + 1) * s.cols)
            for r in range(n):
                for h in range(2):
                    base = ens_peer(r) * s.rows_e + h * s.half
                    value = tmp[pl.ds(pl.multiple_of(base, s.half), s.half), lanes]
                    place(value, acc, snd, (k, h) + relative(r), r, orders[h])
            moves[k] = [start(acc.at[k, h], snd.at[k, h], rcv[0].at[k, h], orders[h], 0) for h in range(2)]

    puts = []

    def latent_part(j):
        at = pl.ds(j * turned, turned)
        glat_s[at, :] = dot_nn(wint[at, :], dpre_s[...]).astype(BF16)
        put = pltpu.make_async_copy(glat_s.at[at], glat_hbm.at[0, at], local_sem.at[3 + s.tiles + j])
        put.start()
        puts.append(put)

    latent_part(0)
    latent_part(1)
    zero = (0,) * nb
    out_moves = []

    def out_step(copy, stage):
        absorb(copy, acc_o, rcv_o[stage], up, stage)
        if stage < nb - 1:
            return start(acc_o, snd_o, rcv_o[stage + 1], up, stage + 1)
        for k in range(nz - 1):
            zsnd_o[k] = acc_o[zero + (k,)].astype(BF16)
            out_moves.append(remote(zsnd_o.at[k], zrcv_o.at[k], {"grid": chip_at(k) * 2 + core}))
        return None

    out_copy = out_step(out_copy, 0)
    latent_part(2)
    latent_part(3)
    for step in range(nz + nb - 1):
        for stage in range(nb):
            k = step - stage
            if not 0 <= k < nz:
                continue
            for h, order in enumerate(orders):
                absorb(moves[k][h], acc.at[k, h], rcv[stage].at[k, h], order, stage)
                if stage < nb - 1:
                    moves[k][h] = start(acc.at[k, h], snd.at[k, h], rcv[stage + 1].at[k, h], order, stage + 1)
            if stage == nb - 1 and k < nz - 1:
                zsnd[k] = acc[(k, slice(None)) + zero].astype(BF16)
                moves[k] = remote(zsnd.at[k], zrcv.at[k], {"grid": chip_at(k) * 2 + core})
        if step + 1 < nb:
            out_copy = out_step(out_copy, step + 1)

    ratio = float(1.0 / np.sqrt(np.float32(ng * s.pts) * np.float32(n)))
    block = acc_o[zero + (nz - 1,)]
    for k in range(nz - 1):
        out_moves[k].wait_recv()
        block = block + zrcv_o[k].astype(F32)
    gall[mine, :] = ratio * block
    gathers = [remote(gall.at[mine], gall.at[mine], ens_peers[r]) for r in range(1, n)]
    block = acc[(nz - 1, slice(None)) + zero]
    for k in range(nz - 1):
        moves[k].wait_recv()
        block = block + zrcv[k].astype(F32)
    gin_ref[...] = (ratio * block).reshape(s.rows_e, s.cols)
    for copy in loss_copies:
        copy.wait_recv()
    loss = loss_g[0]
    for o in range(1, ng):
        loss = loss + loss_g[o]
    loss_ref[...] = loss[0:1, 0:1] * scale
    for copy in gathers:
        copy.wait_recv()
    gout_ref[...] = gall[0:s.nvars, :]
    for copy in sent:
        copy.wait_send()
    for put in puts:
        put.wait()


def hand_out(a, b, c, a_out, b_out, c_out, sem):
    copies = [pltpu.make_async_copy(x, y, sem.at[i]) for i, (x, y) in enumerate(((a, a_out), (b, b_out), (c, c_out)))]
    for copy in copies:
        copy.start()
    for copy in copies:
        copy.wait()


def per_device(n, ng, latent, w_in, w_out, target, area, var_weight):
    hid, lat = w_in.shape
    pts = latent.shape[2]
    nvars = w_out.shape[0]
    s = Sizes(n, ng, hid, lat, nvars, pts)
    nz, nb, cols = s.nz, s.nb, s.cols
    cube = (2,) * nb
    group = max(1, min(nz, 256 // cols))
    vmem = pl.BlockSpec(memory_space=pltpu.VMEM)
    anywhere = pl.BlockSpec(memory_space=pl.ANY)
    scratch = [
        pltpu.VMEM((nz, 2, cols, pts), BF16),
        pltpu.VMEM((nz, cols, pts), BF16),
        pltpu.VMEM((hid, lat), BF16),
        pltpu.VMEM((lat, hid), BF16),
        pltpu.VMEM((nvars, hid), BF16),
        pltpu.VMEM((nvars, pts), F32),
        pltpu.VMEM((s.vpad, hid), F32),
        pltpu.VMEM((s.vpad, hid), BF16),
        pltpu.VMEM((hid, s.vpad), BF16),
        pltpu.VMEM((nz, 2, cols, pts), BF16),
        pltpu.VMEM((nz, cols, pts), BF16),
        pltpu.VMEM((hid, pts), F32),
        pltpu.VMEM((n, s.vrow, pts), F32),
        pltpu.VMEM((n, s.vrow, pts), F32),
        pltpu.VMEM((s.vpad, pts), F32),
        pltpu.VMEM((8, s.vpad), F32),
        pltpu.VMEM((s.vpad, 128), F32),
        pltpu.VMEM((ng, 8, 128), F32),
        pltpu.VMEM((n, s.vrow, pts), BF16),
        pltpu.VMEM((n, s.vrow, pts), BF16),
        pltpu.VMEM((n, s.vrow, pts), BF16),
        pltpu.VMEM((n, 8, 128), F32),
        pltpu.VMEM((ng, 8, 128), F32),
        pltpu.VMEM((hid, pts), BF16),
        pltpu.VMEM((hid, pts), BF16),
        pltpu.VMEM((lat, pts), BF16),
        pltpu.VMEM((s.vpad, cols), F32),
        pltpu.VMEM((hid, group * cols), F32),
        pltpu.VMEM((nz, 2) + cube + (s.half, cols), F32),
        pltpu.VMEM((nz, 2) + cube + (s.half, cols), BF16),
        pltpu.VMEM(cube + (nz, s.vrow, cols), F32),
        pltpu.VMEM(cube + (nz, s.vrow, cols), BF16),
        pltpu.VMEM((n, s.vrow, group * cols), F32),
        pltpu.VMEM((nz - 1, 2, s.half, cols), BF16),
        pltpu.VMEM((nz - 1, 2, s.half, cols), BF16),
        pltpu.VMEM((nz - 1, s.vrow, cols), BF16),
        pltpu.VMEM((nz - 1, s.vrow, cols), BF16),
    ]
    scratch += [pltpu.VMEM((nz, 2) + cube[1 + i:] + (s.half, cols), BF16) for i in range(nb)]
    scratch += [pltpu.VMEM(cube[1 + i:] + (nz, s.vrow, cols), BF16) for i in range(nb)]
    scratch += [
        pltpu.SemaphoreType.DMA((s.copies,)),
        pltpu.SemaphoreType.DMA((s.copies,)),
        pltpu.SemaphoreType.DMA((7 + s.tiles,)),
    ]
    loss, grad_lat, grad_in, grad_out = pl.pallas_call(
        functools.partial(kernel, s),
        out_shape=(
            jax.ShapeDtypeStruct((1, 1), F32),
            jax.ShapeDtypeStruct((1, lat, pts), BF16),
            jax.ShapeDtypeStruct((s.rows_e, cols), F32),
            jax.ShapeDtypeStruct((nvars, cols), F32),
        ),
        in_specs=[anywhere, anywhere, anywhere, anywhere, vmem, vmem],
        out_specs=(vmem, anywhere, vmem, vmem),
        scratch_shapes=scratch,
        compiler_params=pltpu.CompilerParams(
            collective_id=0, has_side_effects=True, vmem_limit_bytes=VMEM_BYTES
        ),
        name="crps_backward",
    )(latent.reshape(nz, 2, cols, pts), w_in, w_out, target, area, var_weight)
    grad_lat, grad_in, grad_out = pl.pallas_call(
        hand_out,
        out_shape=tuple(jax.ShapeDtypeStruct(x.shape, x.dtype) for x in (grad_lat, grad_in, grad_out)),
        in_specs=[anywhere] * 3,
        out_specs=(anywhere,) * 3,
        scratch_shapes=[pltpu.SemaphoreType.DMA((3,))],
        compiler_params=pltpu.CompilerParams(vmem_limit_bytes=VMEM_BYTES),
        name="hand_out",
    )(grad_lat, grad_in, grad_out)
    return loss[0, 0], grad_lat, grad_in, grad_out


def solution(mesh):
    in_specs = (P("ens", None, "grid"), P(), P(), P(None, "grid"), P("grid"), P())
    out_specs = (P(), P("ens", None, "grid"), P("ens", "grid"), P(None, "grid"))
    body = functools.partial(per_device, mesh.shape["ens"], mesh.shape["grid"])
    return jax.shard_map(
        body, mesh=mesh, in_specs=in_specs, out_specs=out_specs, check_vma=False
    )
```

```python
import functools

import jax
import jax.numpy as jnp
import numpy as np
from jax import lax
from jax.experimental import pallas as pl
from jax.experimental.pallas import tpu as pltpu
from jax.sharding import PartitionSpec as P

SMOOTH = 0.01
GELU_C = 0.7978845608
GELU_K = 0.044715
F32 = jnp.float32
BF16 = jnp.bfloat16
VMEM_BYTES = 62 * 1024 * 1024


def dot_nn(a, b):
    return jnp.dot(a, b, preferred_element_type=F32)


def dot_nt(a, b):
    return lax.dot_general(a, b, (((1,), (1,)), ((), ())), preferred_element_type=F32)


def dot_tn(a, b):
    return lax.dot_general(a, b, (((0,), (0,)), ((), ())), preferred_element_type=F32)


class Sizes:
    def __init__(self, n, ng, hid, lat, nvars, pts):
        self.n, self.ng, self.hid, self.lat, self.nvars, self.pts = n, ng, hid, lat, nvars, pts
        self.nz = ng // 2
        self.nb = n.bit_length() - 1
        self.cols = lat // ng
        self.rows_e = hid // n
        self.half = self.rows_e // 2
        self.vrow = -(-(-(-nvars // n)) // 16) * 16
        self.vpad = self.vrow * n
        self.tile = max(256, 2 * self.cols)
        self.tiles = hid // self.tile
        self.copies = 3 * ng + 4 * n + 8 + self.tiles + (2 * self.nz + 1) * (self.nb + 1) + 2 * self.nz + n


def stage_index(nb, order, stage, value):
    index = [slice(None)] * nb
    for bit in order[:stage]:
        index[nb - 1 - bit] = 0
    index[nb - 1 - order[stage]] = value
    return tuple(index)


def kernel(
    s,
    lat_hbm, win_hbm, wout_hbm, target_hbm, area_hbm, vw_hbm,
    loss_ref, glat_ref, gin_ref, gout_ref,
    lat_s, latp, win_s, wint, wout_ref, target_ref, area_ref, vw_ref, wo32, wo_s, wot, hid_s, hidp, slope_s, dec_s, dec_in, tgt_s, vrow_s, vcol_s, area_all,
    dout_o, dout_s, doutp, loss_e, loss_g, dpre_s, dprep, gall,
    tmp, acc, snd, acc_o, snd_o, tmp_o, zsnd, zrcv, zsnd_o, zrcv_o, *rest,
):
    nb, n, ng, nz = s.nb, s.n, s.ng, s.nz
    rcv, rcv_o = rest[:nb], rest[nb:2 * nb]
    send_sem, recv_sem, local_sem = rest[2 * nb:]
    me = lax.axis_index("ens")
    g = lax.axis_index("grid")
    core = g % 2
    chip = g // 2
    bits = [(me // (1 << i)) % 2 for i in range(nb)]
    used = [0]

    def ens_peer(r):
        return sum((bits[i] + ((r >> i) & 1) * (1 - 2 * bits[i])) * (1 << i) for i in range(nb))

    def remote(src, dst, device):
        i = used[0]
        used[0] += 1
        copy = pltpu.make_async_remote_copy(
            src_ref=src, dst_ref=dst, send_sem=send_sem.at[i], recv_sem=recv_sem.at[i],
            device_id=device, device_id_type=pl.DeviceIdType.MESH,
        )
        copy.start()
        sent.append(copy)
        return copy

    sent = []
    twin = {"grid": g + 1 - 2 * core}
    ens_peers = [None] + [{"ens": ens_peer(r)} for r in range(1, n)]
    grid_peers = [None] + [{"grid": (g + o) % ng} for o in range(1, ng)]

    def win_tile(i):
        rows = pl.ds(pl.multiple_of(i * s.tile, s.tile), s.tile)
        return pltpu.make_async_copy(win_hbm.at[rows], win_s.at[rows], local_sem.at[3 + i])

    get_lat = pltpu.make_async_copy(lat_hbm, lat_s, local_sem.at[0])
    get_out = pltpu.make_async_copy(wout_hbm, wout_ref, local_sem.at[1])
    get_target = pltpu.make_async_copy(target_hbm, target_ref, local_sem.at[2])
    get_area = pltpu.make_async_copy(area_hbm, area_ref, local_sem.at[3 + s.tiles])
    get_vw = pltpu.make_async_copy(vw_hbm, vw_ref, local_sem.at[4 + s.tiles])
    get_lat.start()
    for i in range(s.tiles):
        win_tile(i).start()
    get_out.start()
    get_area.start()
    get_vw.start()
    get_target.start()
    barrier = pltpu.get_barrier_semaphore()
    for peer in ens_peers[1:] + grid_peers[1:]:
        pl.semaphore_signal(barrier, inc=1, device_id=peer, device_id_type=pl.DeviceIdType.MESH)

    vrow_s[...] = jnp.zeros_like(vrow_s)
    wo32[...] = jnp.zeros_like(wo32)
    tgt_s[...] = jnp.zeros_like(tgt_s)

    get_lat.wait()
    span = s.tile // (2 * s.cols)

    def forward(i, carry):
        rows = pl.ds(pl.multiple_of(i * s.tile, s.tile), s.tile)
        win_tile(i).wait()
        v = dot_nn(win_s[rows, :], lat_s[...].reshape(s.lat, s.pts))
        t = jnp.tanh(GELU_C * (v + GELU_K * v * v * v))
        hid_s[pl.ds(i * span, span)] = (0.5 * v * (1.0 + t)).astype(BF16).reshape(span, 2, s.cols, s.pts)
        slope_s[rows, :] = 0.5 * (1.0 + t) + 0.5 * v * (1.0 - t * t) * GELU_C * (1.0 + 3.0 * GELU_K * v * v)
        return carry

    lax.fori_loop(0, s.tiles, forward, 0)
    get_area.wait()
    get_vw.wait()
    arow = area_ref[...].reshape(1, s.pts)
    area_all[0] = jnp.broadcast_to(jnp.sum(arow, axis=1, keepdims=True), (8, 128))
    vrow_s[0:1, 0:s.nvars] = vw_ref[...].reshape(1, s.nvars)
    get_out.wait()
    wo32[0:s.nvars, :] = wout_ref[...].astype(F32)
    wo_s[...] = wo32[...].astype(BF16)
    dec_s[...] = dot_nn(wo_s[...], hid_s[...].reshape(s.hid, s.pts)).reshape(n, s.vrow, s.pts)
    pl.semaphore_wait(barrier, n + ng - 2)

    dec_copies = [remote(dec_s.at[ens_peer(r)], dec_in.at[r], ens_peers[r]) for r in range(1, n)]
    area_copies = [remote(area_all.at[0], area_all.at[o], grid_peers[o]) for o in range(1, ng)]
    hid_copy = remote(hid_s.at[:, 1 - core], hidp, twin)
    lat_copy = remote(lat_hbm.at[:, 1 - core], latp, twin)
    dec_in[0] = dec_s[me]
    get_target.wait()
    tgt_s[0:s.nvars, :] = target_ref[...]
    wot[...] = wo32[...].T.astype(BF16)
    square = (s.vpad, s.vpad)
    eye = lax.broadcasted_iota(jnp.int32, square, 0) == lax.broadcasted_iota(jnp.int32, square, 1)
    column = jnp.sum(jnp.where(eye, jnp.broadcast_to(vrow_s[0:1, :], square), 0.0), axis=1, keepdims=True)
    vcol_s[...] = jnp.broadcast_to(column, vcol_s.shape)
    mine = pl.ds(pl.multiple_of(me * s.vrow, s.vrow), s.vrow)
    weight = vcol_s[mine, 0:1] * arow
    target = tgt_s[mine, :]
    turned = s.lat // 4

    def turn(j):
        at = pl.ds(j * turned, turned)
        wint[at, :] = win_s[:, at].T

    turn(0)
    turn(1)
    for copy in area_copies:
        copy.wait_recv()
    total = area_all[0]
    for o in range(1, ng):
        total = total + area_all[o]
    total = total[0:1, 0:1]
    scale = 1.0 / (total * float(s.nvars))
    wide = (float(ng * s.pts) * scale) * weight
    for copy in dec_copies:
        copy.wait_recv()
    members = [dec_in[r] for r in range(n)]
    slopes = [None] * n
    pairs = jnp.full((s.vrow, s.pts), float(n) * float(np.sqrt(np.float32(SMOOTH))), F32)
    for m in range(n):
        for k in range(m):
            u = members[m] - members[k]
            q = u * u + SMOOTH
            root = lax.rsqrt(q)
            pairs = pairs + 2.0 * (q * root)
            slope = u * root
            slopes[m] = slope if slopes[m] is None else slopes[m] + slope
            slopes[k] = -slope if slopes[k] is None else slopes[k] - slope
    local = pairs * (-1.0 / (2.0 * n * (n - 1.0)))
    dout_copies = []
    for r in range(n - 1, -1, -1):
        u = members[r] - target
        q = u * u + SMOOTH
        root = lax.rsqrt(q)
        local = local + (q * root) * (1.0 / n)
        d = (wide * (u * root * (1.0 / n) - slopes[r] * (1.0 / (n * (n - 1.0))))).astype(BF16)
        if r:
            dout_o[r] = d
            dout_copies.append(remote(dout_o.at[r], dout_s.at[me], ens_peers[r]))
        else:
            dout_s[me] = d
    part = jnp.sum(jnp.sum(weight * local, axis=1, keepdims=True), axis=0, keepdims=True)
    loss_e[0] = jnp.broadcast_to(part, (8, 128))
    loss_copies = [remote(loss_e.at[0], loss_e.at[r], ens_peers[r]) for r in range(1, n)]

    turn(2)
    turn(3)
    for copy in dout_copies:
        copy.wait_recv()
    dout_copy = remote(dout_s, doutp, twin)
    dout = dout_s[...].reshape(s.vpad, s.pts)
    dpre_copies = []
    for i in range(s.tiles):
        rows = pl.ds(i * s.tile, s.tile)
        dpre_s[rows, :] = (dot_nn(wot[rows, :], dout) * slope_s[rows, :]).astype(BF16)
        dpre_copies.append(remote(dpre_s.at[rows], dprep.at[rows], twin))

    def chip_at(k):
        return (chip + nz - 1 - k) % nz

    up, down = list(range(nb)), list(range(nb))[::-1]

    def relative(r):
        return tuple((r >> (nb - 1 - axis)) & 1 for axis in range(nb))

    def place(value, sums, send, at, r, order):
        if (r >> order[0]) & 1:
            send[at] = value.astype(BF16)
        else:
            sums[at] = value

    def start(sums, send, into, order, stage):
        index = stage_index(nb, order, stage, 1)
        if stage:
            send[index] = sums[index].astype(BF16)
        return remote(send.at[index], into, ens_peers[1 << order[stage]])

    def absorb(copy, sums, into, order, stage):
        copy.wait_recv()
        index = stage_index(nb, order, stage, 0)
        sums[index] = sums[index] + into[...].astype(F32)

    hid_copy.wait_recv()
    dout_copy.wait_recv()
    group = max(1, min(nz, 256 // s.cols))
    wide_rows = (group * s.cols, s.pts)
    doutp_all = doutp[...].reshape(s.vpad, s.pts)
    for first in range(0, nz, group):
        zs = [chip_at(k) for k in range(first, first + group)]
        own = jnp.stack([hid_s[z, core] for z in zs]).reshape(wide_rows)
        other = jnp.stack([hidp[z] for z in zs]).reshape(wide_rows)
        tmp_o[...] = (dot_nt(dout, own) + dot_nt(doutp_all, other)).reshape(n, s.vrow, group * s.cols)
        for r in range(n):
            for k in range(group):
                value = tmp_o[ens_peer(r), :, k * s.cols:(k + 1) * s.cols]
                place(value, acc_o, snd_o, relative(r) + (first + k,), r, up)
    out_copy = start(acc_o, snd_o, rcv_o[0], up, 0)

    moves = [None] * nz
    orders = (up, down)
    lat_copy.wait_recv()
    for first in range(0, nz, group):
        zs = [chip_at(k) for k in range(first, first + group)]
        own = jnp.stack([lat_s[z, core] for z in zs]).reshape(wide_rows)
        other = jnp.stack([latp[z] for z in zs]).reshape(wide_rows)
        for i in range(s.tiles):
            rows = pl.ds(i * s.tile, s.tile)
            tmp[rows, :] = dot_nt(dpre_s[rows, :], own)
        for i in range(s.tiles):
            if first == 0:
                dpre_copies[i].wait_recv()
            rows = pl.ds(i * s.tile, s.tile)
            tmp[rows, :] += dot_nt(dprep[rows, :], other)
        for k in range(first, first + group):
            lanes = slice((k - first) * s.cols, (k - first + 1) * s.cols)
            for r in range(n):
                for h in range(2):
                    base = ens_peer(r) * s.rows_e + h * s.half
                    value = tmp[pl.ds(pl.multiple_of(base, s.half), s.half), lanes]
                    place(value, acc, snd, (k, h) + relative(r), r, orders[h])
            moves[k] = [start(acc.at[k, h], snd.at[k, h], rcv[0].at[k, h], orders[h], 0) for h in range(2)]


    def latent_part(j):
        at = pl.ds(j * turned, turned)
        glat_ref[0, at, :] = dot_nn(wint[at, :], dpre_s[...]).astype(BF16)

    latent_part(0)
    latent_part(1)
    zero = (0,) * nb
    out_moves = []

    def out_step(copy, stage):
        absorb(copy, acc_o, rcv_o[stage], up, stage)
        if stage < nb - 1:
            return start(acc_o, snd_o, rcv_o[stage + 1], up, stage + 1)
        for k in range(nz - 1):
            zsnd_o[k] = acc_o[zero + (k,)].astype(BF16)
            out_moves.append(remote(zsnd_o.at[k], zrcv_o.at[k], {"grid": chip_at(k) * 2 + core}))
        return None

    out_copy = out_step(out_copy, 0)
    latent_part(2)
    latent_part(3)
    for copy in loss_copies:
        copy.wait_recv()
    here = loss_e[0]
    for r in range(1, n):
        here = here + loss_e[r]
    loss_g[0] = here
    loss_copies = [remote(loss_g.at[0], loss_g.at[o], grid_peers[o]) for o in range(1, ng)]
    ratio = float(1.0 / np.sqrt(np.float32(ng * s.pts) * np.float32(n)))
    for step in range(nz + nb - 1):
        for stage in range(nb):
            k = step - stage
            if not 0 <= k < nz:
                continue
            for h, order in enumerate(orders):
                absorb(moves[k][h], acc.at[k, h], rcv[stage].at[k, h], order, stage)
                if stage < nb - 1:
                    moves[k][h] = start(acc.at[k, h], snd.at[k, h], rcv[stage + 1].at[k, h], order, stage + 1)
            if stage == nb - 1 and k < nz - 1:
                zsnd[k] = acc[(k, slice(None)) + zero].astype(BF16)
                moves[k] = remote(zsnd.at[k], zrcv.at[k], {"grid": chip_at(k) * 2 + core})
        if step + 1 < nb:
            out_copy = out_step(out_copy, step + 1)
        if step == nz + nb - 3:
            block = acc_o[zero + (nz - 1,)]
            for k in range(nz - 1):
                out_moves[k].wait_recv()
                block = block + zrcv_o[k].astype(F32)
            gall[mine, :] = ratio * block
            gathers = [remote(gall.at[mine], gall.at[mine], ens_peers[r]) for r in range(1, n)]

    block = acc[(nz - 1, slice(None)) + zero]
    for k in range(nz - 1):
        moves[k].wait_recv()
        block = block + zrcv[k].astype(F32)
    gin_ref[...] = (ratio * block).reshape(s.rows_e, s.cols)
    for copy in loss_copies:
        copy.wait_recv()
    loss = loss_g[0]
    for o in range(1, ng):
        loss = loss + loss_g[o]
    loss_ref[...] = loss[0:1, 0:1] * scale
    for copy in gathers:
        copy.wait_recv()
    gout_ref[...] = gall[0:s.nvars, :]
    for copy in sent:
        copy.wait_send()


def hand_out(a, b, c, a_out, b_out, c_out, sem):
    copies = [pltpu.make_async_copy(x, y, sem.at[i]) for i, (x, y) in enumerate(((a, a_out), (b, b_out), (c, c_out)))]
    for copy in copies:
        copy.start()
    for copy in copies:
        copy.wait()


def per_device(n, ng, latent, w_in, w_out, target, area, var_weight):
    hid, lat = w_in.shape
    pts = latent.shape[2]
    nvars = w_out.shape[0]
    s = Sizes(n, ng, hid, lat, nvars, pts)
    nz, nb, cols = s.nz, s.nb, s.cols
    cube = (2,) * nb
    group = max(1, min(nz, 256 // cols))
    vmem = pl.BlockSpec(memory_space=pltpu.VMEM)
    hbm = pl.BlockSpec(memory_space=pltpu.HBM)
    scratch = [
        pltpu.VMEM((nz, 2, cols, pts), BF16),
        pltpu.VMEM((nz, cols, pts), BF16),
        pltpu.VMEM((hid, lat), BF16),
        pltpu.VMEM((lat, hid), BF16),
        pltpu.VMEM((nvars, hid), BF16),
        pltpu.VMEM((nvars, pts), F32),
        pltpu.VMEM((pts,), F32),
        pltpu.VMEM((nvars,), F32),
        pltpu.VMEM((s.vpad, hid), F32),
        pltpu.VMEM((s.vpad, hid), BF16),
        pltpu.VMEM((hid, s.vpad), BF16),
        pltpu.VMEM((nz, 2, cols, pts), BF16),
        pltpu.VMEM((nz, cols, pts), BF16),
        pltpu.VMEM((hid, pts), F32),
        pltpu.VMEM((n, s.vrow, pts), F32),
        pltpu.VMEM((n, s.vrow, pts), F32),
        pltpu.VMEM((s.vpad, pts), F32),
        pltpu.VMEM((8, s.vpad), F32),
        pltpu.VMEM((s.vpad, 128), F32),
        pltpu.VMEM((ng, 8, 128), F32),
        pltpu.VMEM((n, s.vrow, pts), BF16),
        pltpu.VMEM((n, s.vrow, pts), BF16),
        pltpu.VMEM((n, s.vrow, pts), BF16),
        pltpu.VMEM((n, 8, 128), F32),
        pltpu.VMEM((ng, 8, 128), F32),
        pltpu.VMEM((hid, pts), BF16),
        pltpu.VMEM((hid, pts), BF16),
        pltpu.VMEM((s.vpad, cols), F32),
        pltpu.VMEM((hid, group * cols), F32),
        pltpu.VMEM((nz, 2) + cube + (s.half, cols), F32),
        pltpu.VMEM((nz, 2) + cube + (s.half, cols), BF16),
        pltpu.VMEM(cube + (nz, s.vrow, cols), F32),
        pltpu.VMEM(cube + (nz, s.vrow, cols), BF16),
        pltpu.VMEM((n, s.vrow, group * cols), F32),
        pltpu.VMEM((nz - 1, 2, s.half, cols), BF16),
        pltpu.VMEM((nz - 1, 2, s.half, cols), BF16),
        pltpu.VMEM((nz - 1, s.vrow, cols), BF16),
        pltpu.VMEM((nz - 1, s.vrow, cols), BF16),
    ]
    scratch += [pltpu.VMEM((nz, 2) + cube[1 + i:] + (s.half, cols), BF16) for i in range(nb)]
    scratch += [pltpu.VMEM(cube[1 + i:] + (nz, s.vrow, cols), BF16) for i in range(nb)]
    scratch += [
        pltpu.SemaphoreType.DMA((s.copies,)),
        pltpu.SemaphoreType.DMA((s.copies,)),
        pltpu.SemaphoreType.DMA((5 + s.tiles,)),
    ]
    loss, grad_lat, grad_in, grad_out = pl.pallas_call(
        functools.partial(kernel, s),
        out_shape=(
            jax.ShapeDtypeStruct((1, 1), F32),
            jax.ShapeDtypeStruct((1, lat, pts), BF16),
            jax.ShapeDtypeStruct((s.rows_e, cols), F32),
            jax.ShapeDtypeStruct((nvars, cols), F32),
        ),
        in_specs=[hbm] * 6,
        out_specs=(vmem,) * 4,
        scratch_shapes=scratch,
        compiler_params=pltpu.CompilerParams(
            collective_id=0, has_side_effects=True, vmem_limit_bytes=VMEM_BYTES
        ),
        name="crps_backward",
    )(latent.reshape(nz, 2, cols, pts), w_in, w_out, target, area, var_weight)
    grad_lat, grad_in, grad_out = pl.pallas_call(
        hand_out,
        out_shape=tuple(jax.ShapeDtypeStruct(x.shape, x.dtype) for x in (grad_lat, grad_in, grad_out)),
        in_specs=[vmem] * 3,
        out_specs=(hbm,) * 3,
        scratch_shapes=[pltpu.SemaphoreType.DMA((3,))],
        compiler_params=pltpu.CompilerParams(vmem_limit_bytes=VMEM_BYTES),
        name="hand_out",
    )(grad_lat, grad_in, grad_out)
    return loss[0, 0], grad_lat, grad_in, grad_out


def solution(mesh):
    in_specs = (P("ens", None, "grid"), P(), P(), P(None, "grid"), P("grid"), P())
    out_specs = (P(), P("ens", None, "grid"), P("ens", "grid"), P(None, "grid"))
    body = functools.partial(per_device, mesh.shape["ens"], mesh.shape["grid"])
    return jax.shard_map(
        body, mesh=mesh, in_specs=in_specs, out_specs=out_specs, check_vma=False
    )
```

```python
import functools

import jax
import jax.numpy as jnp
import numpy as np
from jax import lax
from jax.experimental import pallas as pl
from jax.experimental.pallas import tpu as pltpu
from jax.sharding import PartitionSpec as P

SMOOTH = 0.01
GELU_C = 0.7978845608
GELU_K = 0.044715
F32 = jnp.float32
BF16 = jnp.bfloat16
VMEM_BYTES = 62 * 1024 * 1024


def dot_nn(a, b):
    return jnp.dot(a, b, preferred_element_type=F32)


def dot_nt(a, b):
    return lax.dot_general(a, b, (((1,), (1,)), ((), ())), preferred_element_type=F32)


def dot_tn(a, b):
    return lax.dot_general(a, b, (((0,), (0,)), ((), ())), preferred_element_type=F32)


class Sizes:
    def __init__(self, n, ng, hid, lat, nvars, pts):
        self.n, self.ng, self.hid, self.lat, self.nvars, self.pts = n, ng, hid, lat, nvars, pts
        self.nz = ng // 2
        self.nb = n.bit_length() - 1
        self.cols = lat // ng
        self.rows_e = hid // n
        self.half = self.rows_e // 2
        self.vrow = -(-(-(-nvars // n)) // 16) * 16
        self.vpad = self.vrow * n
        self.tile = max(256, 2 * self.cols)
        self.tiles = hid // self.tile
        self.copies = 3 * ng + 4 * n + 8 + self.tiles + (2 * self.nz + 1) * (self.nb + 1) + 2 * self.nz + n


def stage_index(nb, order, stage, value):
    index = [slice(None)] * nb
    for bit in order[:stage]:
        index[nb - 1 - bit] = 0
    index[nb - 1 - order[stage]] = value
    return tuple(index)


def kernel(
    s,
    lat_hbm, win_hbm, wout_hbm, target_hbm, area_hbm, vw_hbm,
    loss_ref, glat_ref, gin_ref, gout_ref,
    lat_s, latp, win_s, wout_ref, target_ref, area_ref, vw_ref, wo32, wo_s, wot, hid_s, hidp, pre_s, slope_s, dec_s, dec_in, tgt_s, vrow_s, vcol_s, area_all,
    dout_o, dout_s, doutp, loss_e, loss_g, dpre_s, dprep, gall,
    tmp, acc, snd, acc_o, snd_o, tmp_o, zsnd, zrcv, zsnd_o, zrcv_o, *rest,
):
    nb, n, ng, nz = s.nb, s.n, s.ng, s.nz
    rcv, rcv_o = rest[:nb], rest[nb:2 * nb]
    send_sem, recv_sem, local_sem = rest[2 * nb:]
    me = lax.axis_index("ens")
    g = lax.axis_index("grid")
    core = g % 2
    chip = g // 2
    bits = [(me // (1 << i)) % 2 for i in range(nb)]
    used = [0]

    def ens_peer(r):
        return sum((bits[i] + ((r >> i) & 1) * (1 - 2 * bits[i])) * (1 << i) for i in range(nb))

    def remote(src, dst, device):
        i = used[0]
        used[0] += 1
        copy = pltpu.make_async_remote_copy(
            src_ref=src, dst_ref=dst, send_sem=send_sem.at[i], recv_sem=recv_sem.at[i],
            device_id=device, device_id_type=pl.DeviceIdType.MESH,
        )
        copy.start()
        sent.append(copy)
        return copy

    sent = []
    twin = {"grid": g + 1 - 2 * core}
    ens_peers = [None] + [{"ens": ens_peer(r)} for r in range(1, n)]
    grid_peers = [None] + [{"grid": (g + o) % ng} for o in range(1, ng)]

    def win_tile(i):
        rows = pl.ds(i * s.tile, s.tile)
        return pltpu.make_async_copy(win_hbm.at[rows], win_s.at[rows], local_sem.at[3 + i])

    get_lat = pltpu.make_async_copy(lat_hbm, lat_s, local_sem.at[0])
    get_out = pltpu.make_async_copy(wout_hbm, wout_ref, local_sem.at[1])
    get_target = pltpu.make_async_copy(target_hbm, target_ref, local_sem.at[2])
    get_area = pltpu.make_async_copy(area_hbm, area_ref, local_sem.at[3 + s.tiles])
    get_vw = pltpu.make_async_copy(vw_hbm, vw_ref, local_sem.at[4 + s.tiles])
    get_area.start()
    get_vw.start()
    get_out.start()
    get_lat.start()
    for i in range(s.tiles):
        win_tile(i).start()
    get_target.start()
    barrier = pltpu.get_barrier_semaphore()
    for peer in ens_peers[1:] + grid_peers[1:]:
        pl.semaphore_signal(barrier, inc=1, device_id=peer, device_id_type=pl.DeviceIdType.MESH)

    vrow_s[...] = jnp.zeros_like(vrow_s)
    wo32[...] = jnp.zeros_like(wo32)
    tgt_s[...] = jnp.zeros_like(tgt_s)

    get_area.wait()
    get_vw.wait()
    arow = area_ref[...].reshape(1, s.pts)
    area_all[0] = jnp.broadcast_to(jnp.sum(arow, axis=1, keepdims=True), (8, 128))
    vrow_s[0:1, 0:s.nvars] = vw_ref[...].reshape(1, s.nvars)
    get_out.wait()
    wo32[0:s.nvars, :] = wout_ref[...].astype(F32)
    wo_s[...] = wo32[...].astype(BF16)

    get_lat.wait()
    span = s.tile // (2 * s.cols)

    for i in range(s.tiles):
        rows = pl.ds(i * s.tile, s.tile)
        win_tile(i).wait()
        v = dot_nn(win_s[rows, :], lat_s[...].reshape(s.lat, s.pts))
        t = jnp.tanh(GELU_C * (v + GELU_K * v * v * v))
        hid_s[pl.ds(i * span, span)] = (0.5 * v * (1.0 + t)).astype(BF16).reshape(span, 2, s.cols, s.pts)
        pre_s[rows, :] = v
        slope_s[rows, :] = t
    dec_s[...] = dot_nn(wo_s[...], hid_s[...].reshape(s.hid, s.pts)).reshape(n, s.vrow, s.pts)
    pl.semaphore_wait(barrier, n + ng - 2)

    dec_copies = [remote(dec_s.at[ens_peer(r)], dec_in.at[r], ens_peers[r]) for r in range(1, n)]
    area_copies = [remote(area_all.at[0], area_all.at[o], grid_peers[o]) for o in range(1, ng)]
    hid_copy = remote(hid_s.at[:, 1 - core], hidp, twin)
    lat_copy = remote(lat_hbm.at[:, 1 - core], latp, twin)
    dec_in[0] = dec_s[me]
    get_target.wait()
    tgt_s[0:s.nvars, :] = target_ref[...]
    wot[...] = wo32[...].T.astype(BF16)
    square = (s.vpad, s.vpad)
    eye = lax.broadcasted_iota(jnp.int32, square, 0) == lax.broadcasted_iota(jnp.int32, square, 1)
    column = jnp.sum(jnp.where(eye, jnp.broadcast_to(vrow_s[0:1, :], square), 0.0), axis=1, keepdims=True)
    vcol_s[...] = jnp.broadcast_to(column, vcol_s.shape)
    mine = pl.ds(pl.multiple_of(me * s.vrow, s.vrow), s.vrow)
    weight = vcol_s[mine, 0:1] * arow
    target = tgt_s[mine, :]
    for i in range(s.tiles):
        rows = pl.ds(i * s.tile, s.tile)
        v, t = pre_s[rows, :], slope_s[rows, :]
        slope_s[rows, :] = 0.5 * (1.0 + t) + 0.5 * v * (1.0 - t * t) * GELU_C * (1.0 + 3.0 * GELU_K * v * v)
    for copy in area_copies:
        copy.wait_recv()
    total = area_all[0]
    for o in range(1, ng):
        total = total + area_all[o]
    total = total[0:1, 0:1]
    scale = 1.0 / (total * float(s.nvars))
    wide = (float(ng * s.pts) * scale) * weight
    for copy in dec_copies:
        copy.wait_recv()
    members = [dec_in[r] for r in range(n)]
    slopes = [None] * n
    pairs = jnp.full((s.vrow, s.pts), float(n) * float(np.sqrt(np.float32(SMOOTH))), F32)
    for m in range(n):
        for k in range(m):
            u = members[m] - members[k]
            q = u * u + SMOOTH
            root = lax.rsqrt(q)
            pairs = pairs + 2.0 * (q * root)
            slope = u * root
            slopes[m] = slope if slopes[m] is None else slopes[m] + slope
            slopes[k] = -slope if slopes[k] is None else slopes[k] - slope
    local = pairs * (-1.0 / (2.0 * n * (n - 1.0)))
    dout_copies = []
    for r in range(n - 1, -1, -1):
        u = members[r] - target
        q = u * u + SMOOTH
        root = lax.rsqrt(q)
        local = local + (q * root) * (1.0 / n)
        d = (wide * (u * root * (1.0 / n) - slopes[r] * (1.0 / (n * (n - 1.0))))).astype(BF16)
        if r:
            dout_o[r] = d
            dout_copies.append(remote(dout_o.at[r], dout_s.at[me], ens_peers[r]))
        else:
            dout_s[me] = d
    part = jnp.sum(jnp.sum(weight * local, axis=1, keepdims=True), axis=0, keepdims=True)
    loss_e[0] = jnp.broadcast_to(part, (8, 128))
    loss_copies = [remote(loss_e.at[0], loss_e.at[r], ens_peers[r]) for r in range(1, n)]

    for copy in dout_copies:
        copy.wait_recv()
    dout_copy = remote(dout_s, doutp, twin)
    dout = dout_s[...].reshape(s.vpad, s.pts)
    dpre_copies = []
    for i in range(s.tiles):
        rows = pl.ds(i * s.tile, s.tile)
        dpre_s[rows, :] = (dot_nn(wot[rows, :], dout) * slope_s[rows, :]).astype(BF16)
        dpre_copies.append(remote(dpre_s.at[rows], dprep.at[rows], twin))

    def chip_at(k):
        return (chip + nz - 1 - k) % nz

    up, down = list(range(nb)), list(range(nb))[::-1]

    def relative(r):
        return tuple((r >> (nb - 1 - axis)) & 1 for axis in range(nb))

    def place(value, sums, send, at, r, order):
        if (r >> order[0]) & 1:
            send[at] = value.astype(BF16)
        else:
            sums[at] = value

    def start(sums, send, into, order, stage):
        index = stage_index(nb, order, stage, 1)
        if stage:
            send[index] = sums[index].astype(BF16)
        return remote(send.at[index], into, ens_peers[1 << order[stage]])

    def absorb(copy, sums, into, order, stage):
        copy.wait_recv()
        index = stage_index(nb, order, stage, 0)
        sums[index] = sums[index] + into[...].astype(F32)

    hid_copy.wait_recv()
    dout_copy.wait_recv()
    group = max(1, min(nz, 256 // s.cols))
    wide_rows = (group * s.cols, s.pts)
    doutp_all = doutp[...].reshape(s.vpad, s.pts)
    for first in range(0, nz, group):
        zs = [chip_at(k) for k in range(first, first + group)]
        own = jnp.stack([hid_s[z, core] for z in zs]).reshape(wide_rows)
        other = jnp.stack([hidp[z] for z in zs]).reshape(wide_rows)
        tmp_o[...] = (dot_nt(dout, own) + dot_nt(doutp_all, other)).reshape(n, s.vrow, group * s.cols)
        for r in range(n):
            for k in range(group):
                value = tmp_o[ens_peer(r), :, k * s.cols:(k + 1) * s.cols]
                place(value, acc_o, snd_o, relative(r) + (first + k,), r, up)
    out_copy = start(acc_o, snd_o, rcv_o[0], up, 0)

    moves = [None] * nz
    orders = (up, down)
    lat_copy.wait_recv()
    for first in range(0, nz, group):
        zs = [chip_at(k) for k in range(first, first + group)]
        own = jnp.stack([lat_s[z, core] for z in zs]).reshape(wide_rows)
        other = jnp.stack([latp[z] for z in zs]).reshape(wide_rows)
        for i in range(s.tiles):
            rows = pl.ds(i * s.tile, s.tile)
            tmp[rows, :] = dot_nt(dpre_s[rows, :], own)
        for i in range(s.tiles):
            if first == 0:
                dpre_copies[i].wait_recv()
            rows = pl.ds(i * s.tile, s.tile)
            tmp[rows, :] += dot_nt(dprep[rows, :], other)
        for k in range(first, first + group):
            lanes = slice((k - first) * s.cols, (k - first + 1) * s.cols)
            for r in range(n):
                for h in range(2):
                    base = ens_peer(r) * s.rows_e + h * s.half
                    value = tmp[pl.ds(pl.multiple_of(base, s.half), s.half), lanes]
                    place(value, acc, snd, (k, h) + relative(r), r, orders[h])
            moves[k] = [start(acc.at[k, h], snd.at[k, h], rcv[0].at[k, h], orders[h], 0) for h in range(2)]


    quarter = s.lat // 4

    def latent_part(j):
        at = pl.ds(j * quarter, quarter)
        glat_ref[0, at, :] = dot_tn(win_s[:, at], dpre_s[...]).astype(BF16)

    latent_part(0)
    zero = (0,) * nb
    out_moves = []

    def out_step(copy, stage):
        absorb(copy, acc_o, rcv_o[stage], up, stage)
        if stage < nb - 1:
            return start(acc_o, snd_o, rcv_o[stage + 1], up, stage + 1)
        for k in range(nz - 1):
            zsnd_o[k] = acc_o[zero + (k,)].astype(BF16)
            out_moves.append(remote(zsnd_o.at[k], zrcv_o.at[k], {"grid": chip_at(k) * 2 + core}))
        return None

    out_copy = out_step(out_copy, 0)
    latent_part(1)
    for copy in loss_copies:
        copy.wait_recv()
    here = loss_e[0]
    for r in range(1, n):
        here = here + loss_e[r]
    loss_g[0] = here
    loss_copies = [remote(loss_g.at[0], loss_g.at[o], grid_peers[o]) for o in range(1, ng)]
    ratio = float(1.0 / np.sqrt(np.float32(ng * s.pts) * np.float32(n)))
    early = len(sent)
    for step in range(nz + nb - 1):
        if step in (1, 2):
            latent_part(step + 1)
        for stage in range(nb):
            k = step - stage
            if not 0 <= k < nz:
                continue
            for h, order in enumerate(orders):
                absorb(moves[k][h], acc.at[k, h], rcv[stage].at[k, h], order, stage)
                if stage < nb - 1:
                    moves[k][h] = start(acc.at[k, h], snd.at[k, h], rcv[stage + 1].at[k, h], order, stage + 1)
            if stage == nb - 1 and k < nz - 1:
                zsnd[k] = acc[(k, slice(None)) + zero].astype(BF16)
                moves[k] = remote(zsnd.at[k], zrcv.at[k], {"grid": chip_at(k) * 2 + core})
        if step + 1 < nb:
            out_copy = out_step(out_copy, step + 1)
        if step == 2:
            for copy in sent[:early]:
                copy.wait_send()
        if step == nz + nb - 3:
            block = acc_o[zero + (nz - 1,)]
            for k in range(nz - 1):
                out_moves[k].wait_recv()
                block = block + zrcv_o[k].astype(F32)
            gall[mine, :] = ratio * block
            gathers = [remote(gall.at[mine], gall.at[mine], ens_peers[r]) for r in range(1, n)]

    block = acc[(nz - 1, slice(None)) + zero]
    for k in range(nz - 1):
        moves[k].wait_recv()
        block = block + zrcv[k].astype(F32)
    gin_ref[...] = (ratio * block).reshape(s.rows_e, s.cols)
    for copy in loss_copies:
        copy.wait_recv()
    loss = loss_g[0]
    for o in range(1, ng):
        loss = loss + loss_g[o]
    loss_ref[...] = loss[0:1, 0:1] * scale
    for copy in gathers:
        copy.wait_recv()
    gout_ref[...] = gall[0:s.nvars, :]
    for copy in sent[early:]:
        copy.wait_send()


def hand_out(*refs):
    sources, targets, held, sems = refs[:3], refs[3:6], refs[6:9], refs[9]
    reads = [pltpu.make_async_copy(x, y, sems.at[0, i]) for i, (x, y) in enumerate(zip(sources, held))]
    writes = [pltpu.make_async_copy(x, y, sems.at[1, i]) for i, (x, y) in enumerate(zip(held, targets))]
    for copy in reads:
        copy.start()
    for read, write in zip(reads, writes):
        read.wait()
        write.start()
    for copy in writes:
        copy.wait()


def per_device(n, ng, latent, w_in, w_out, target, area, var_weight):
    hid, lat = w_in.shape
    pts = latent.shape[2]
    nvars = w_out.shape[0]
    s = Sizes(n, ng, hid, lat, nvars, pts)
    nz, nb, cols = s.nz, s.nb, s.cols
    cube = (2,) * nb
    group = max(1, min(nz, 256 // cols))
    vmem = pl.BlockSpec(memory_space=pltpu.VMEM)
    hbm = pl.BlockSpec(memory_space=pltpu.HBM)
    scratch = [
        pltpu.VMEM((nz, 2, cols, pts), BF16),
        pltpu.VMEM((nz, cols, pts), BF16),
        pltpu.VMEM((hid, lat), BF16),
        pltpu.VMEM((nvars, hid), BF16),
        pltpu.VMEM((nvars, pts), F32),
        pltpu.VMEM((pts,), F32),
        pltpu.VMEM((nvars,), F32),
        pltpu.VMEM((s.vpad, hid), F32),
        pltpu.VMEM((s.vpad, hid), BF16),
        pltpu.VMEM((hid, s.vpad), BF16),
        pltpu.VMEM((nz, 2, cols, pts), BF16),
        pltpu.VMEM((nz, cols, pts), BF16),
        pltpu.VMEM((hid, pts), F32),
        pltpu.VMEM((hid, pts), F32),
        pltpu.VMEM((n, s.vrow, pts), F32),
        pltpu.VMEM((n, s.vrow, pts), F32),
        pltpu.VMEM((s.vpad, pts), F32),
        pltpu.VMEM((8, s.vpad), F32),
        pltpu.VMEM((s.vpad, 128), F32),
        pltpu.VMEM((ng, 8, 128), F32),
        pltpu.VMEM((n, s.vrow, pts), BF16),
        pltpu.VMEM((n, s.vrow, pts), BF16),
        pltpu.VMEM((n, s.vrow, pts), BF16),
        pltpu.VMEM((n, 8, 128), F32),
        pltpu.VMEM((ng, 8, 128), F32),
        pltpu.VMEM((hid, pts), BF16),
        pltpu.VMEM((hid, pts), BF16),
        pltpu.VMEM((s.vpad, cols), F32),
        pltpu.VMEM((hid, group * cols), F32),
        pltpu.VMEM((nz, 2) + cube + (s.half, cols), F32),
        pltpu.VMEM((nz, 2) + cube + (s.half, cols), BF16),
        pltpu.VMEM(cube + (nz, s.vrow, cols), F32),
        pltpu.VMEM(cube + (nz, s.vrow, cols), BF16),
        pltpu.VMEM((n, s.vrow, group * cols), F32),
        pltpu.VMEM((nz - 1, 2, s.half, cols), BF16),
        pltpu.VMEM((nz - 1, 2, s.half, cols), BF16),
        pltpu.VMEM((nz - 1, s.vrow, cols), BF16),
        pltpu.VMEM((nz - 1, s.vrow, cols), BF16),
    ]
    scratch += [pltpu.VMEM((nz, 2) + cube[1 + i:] + (s.half, cols), BF16) for i in range(nb)]
    scratch += [pltpu.VMEM(cube[1 + i:] + (nz, s.vrow, cols), BF16) for i in range(nb)]
    scratch += [
        pltpu.SemaphoreType.DMA((s.copies,)),
        pltpu.SemaphoreType.DMA((s.copies,)),
        pltpu.SemaphoreType.DMA((5 + s.tiles,)),
    ]
    loss, grad_lat, grad_in, grad_out = pl.pallas_call(
        functools.partial(kernel, s),
        out_shape=(
            jax.ShapeDtypeStruct((1, 1), F32),
            jax.ShapeDtypeStruct((1, lat, pts), BF16),
            jax.ShapeDtypeStruct((s.rows_e, cols), F32),
            jax.ShapeDtypeStruct((nvars, cols), F32),
        ),
        in_specs=[hbm] * 6,
        out_specs=(vmem,) * 4,
        scratch_shapes=scratch,
        compiler_params=pltpu.CompilerParams(
            collective_id=0, has_side_effects=True, vmem_limit_bytes=VMEM_BYTES
        ),
        name="crps_backward",
    )(latent.reshape(nz, 2, cols, pts), w_in, w_out, target, area, var_weight)
    grad_lat, grad_in, grad_out = pl.pallas_call(
        hand_out,
        out_shape=tuple(jax.ShapeDtypeStruct(x.shape, x.dtype) for x in (grad_lat, grad_in, grad_out)),
        in_specs=[hbm] * 3,
        out_specs=(hbm,) * 3,
        scratch_shapes=[pltpu.VMEM(x.shape, x.dtype) for x in (grad_lat, grad_in, grad_out)]
        + [pltpu.SemaphoreType.DMA((2, 3))],
        compiler_params=pltpu.CompilerParams(vmem_limit_bytes=VMEM_BYTES),
        name="hand_out",
    )(grad_lat, grad_in, grad_out)
    return loss[0, 0], grad_lat, grad_in, grad_out


def solution(mesh):
    in_specs = (P("ens", None, "grid"), P(), P(), P(None, "grid"), P("grid"), P())
    out_specs = (P(), P("ens", None, "grid"), P("ens", "grid"), P(None, "grid"))
    body = functools.partial(per_device, mesh.shape["ens"], mesh.shape["grid"])
    return jax.shard_map(
        body, mesh=mesh, in_specs=in_specs, out_specs=out_specs, check_vma=False
    )
```

```python
import functools

import jax
import jax.numpy as jnp
import numpy as np
from jax import lax
from jax.experimental import pallas as pl
from jax.experimental.pallas import tpu as pltpu
from jax.sharding import PartitionSpec as P

SMOOTH = 0.01
GELU_C = 0.7978845608
GELU_K = 0.044715
F32 = jnp.float32
BF16 = jnp.bfloat16
VMEM_BYTES = 62 * 1024 * 1024
AHEAD = 2


def dot_nn(a, b):
    return jnp.dot(a, b, preferred_element_type=F32)


def dot_nt(a, b):
    return lax.dot_general(a, b, (((1,), (1,)), ((), ())), preferred_element_type=F32)


def dot_tn(a, b):
    return lax.dot_general(a, b, (((0,), (0,)), ((), ())), preferred_element_type=F32)


class Sizes:
    def __init__(self, n, ng, hid, lat, nvars, pts):
        self.n, self.ng, self.hid, self.lat, self.nvars, self.pts = n, ng, hid, lat, nvars, pts
        self.nz = ng // 2
        self.nb = n.bit_length() - 1
        self.cols = lat // ng
        self.rows_e = hid // n
        self.half = self.rows_e // 2
        self.vrow = -(-(-(-nvars // n)) // 16) * 16
        self.vpad = self.vrow * n
        self.tile = max(256, 2 * self.cols)
        self.tiles = hid // self.tile
        self.copies = 3 * ng + 4 * n + 8 + self.tiles + (2 * self.nz + 1) * (self.nb + 1) + 2 * self.nz + n


def stage_index(nb, order, stage, value):
    index = [slice(None)] * nb
    for bit in order[:stage]:
        index[nb - 1 - bit] = 0
    index[nb - 1 - order[stage]] = value
    return tuple(index)


def kernel(
    s,
    lat_hbm, win_hbm, wout_hbm, target_hbm, area_hbm, vw_hbm,
    loss_ref, glat_ref, gin_ref, gout_ref,
    lat_s, latp, win_s, wout_ref, target_ref, area_ref, vw_ref, wo32, wo_s, wot, hid_s, hidp, pre_s, slope_s, dec_s, dec_in, tgt_s, vrow_s, vcol_s, area_all,
    dout_o, dout_s, doutp, loss_e, loss_g, dpre_s, dprep, gall,
    tmp, acc, snd, acc_o, snd_o, tmp_o, zsnd, zrcv, zsnd_o, zrcv_o, *rest,
):
    nb, n, ng, nz = s.nb, s.n, s.ng, s.nz
    rcv, rcv_o = rest[:nb], rest[nb:2 * nb]
    send_sem, recv_sem, local_sem = rest[2 * nb:]
    me = lax.axis_index("ens")
    g = lax.axis_index("grid")
    core = g % 2
    chip = g // 2
    bits = [(me // (1 << i)) % 2 for i in range(nb)]
    used = [0]

    def ens_peer(r):
        return sum((bits[i] + ((r >> i) & 1) * (1 - 2 * bits[i])) * (1 << i) for i in range(nb))

    def remote(src, dst, device):
        i = used[0]
        used[0] += 1
        copy = pltpu.make_async_remote_copy(
            src_ref=src, dst_ref=dst, send_sem=send_sem.at[i], recv_sem=recv_sem.at[i],
            device_id=device, device_id_type=pl.DeviceIdType.MESH,
        )
        copy.start()
        sent.append(copy)
        return copy

    sent = []
    twin = {"grid": g + 1 - 2 * core}
    ens_peers = [None] + [{"ens": ens_peer(r)} for r in range(1, n)]
    grid_peers = [None] + [{"grid": (g + o) % ng} for o in range(1, ng)]

    def win_tile(i):
        rows = pl.ds(i * s.tile, s.tile)
        return pltpu.make_async_copy(win_hbm.at[rows], win_s.at[rows], local_sem.at[3 + i])

    get_lat = pltpu.make_async_copy(lat_hbm, lat_s, local_sem.at[0])
    get_out = pltpu.make_async_copy(wout_hbm, wout_ref, local_sem.at[1])
    get_target = pltpu.make_async_copy(target_hbm, target_ref, local_sem.at[2])
    get_area = pltpu.make_async_copy(area_hbm, area_ref, local_sem.at[3 + s.tiles])
    get_vw = pltpu.make_async_copy(vw_hbm, vw_ref, local_sem.at[4 + s.tiles])
    get_area.start()
    get_vw.start()
    get_out.start()
    get_lat.start()
    for i in range(s.tiles):
        win_tile(i).start()
    get_target.start()
    barrier = pltpu.get_barrier_semaphore()
    for peer in ens_peers[1:] + grid_peers[1:]:
        pl.semaphore_signal(barrier, inc=1, device_id=peer, device_id_type=pl.DeviceIdType.MESH)

    vrow_s[...] = jnp.zeros_like(vrow_s)
    wo32[...] = jnp.zeros_like(wo32)
    tgt_s[...] = jnp.zeros_like(tgt_s)

    get_area.wait()
    get_vw.wait()
    arow = area_ref[...].reshape(1, s.pts)
    area_all[0] = jnp.broadcast_to(jnp.sum(arow, axis=1, keepdims=True), (8, 128))
    vrow_s[0:1, 0:s.nvars] = vw_ref[...].reshape(1, s.nvars)
    get_out.wait()
    wo32[0:s.nvars, :] = wout_ref[...].astype(F32)
    wo_s[...] = wo32[...].astype(BF16)

    get_lat.wait()
    span = s.tile // (2 * s.cols)

    for i in range(s.tiles):
        rows = pl.ds(i * s.tile, s.tile)
        win_tile(i).wait()
        v = dot_nn(win_s[rows, :], lat_s[...].reshape(s.lat, s.pts))
        t = jnp.tanh(GELU_C * (v + GELU_K * v * v * v))
        hid_s[pl.ds(i * span, span)] = (0.5 * v * (1.0 + t)).astype(BF16).reshape(span, 2, s.cols, s.pts)
        pre_s[rows, :] = v
        slope_s[rows, :] = t
    dec_s[...] = dot_nn(wo_s[...], hid_s[...].reshape(s.hid, s.pts)).reshape(n, s.vrow, s.pts)
    pl.semaphore_wait(barrier, n + ng - 2)

    dec_copies = [remote(dec_s.at[ens_peer(r)], dec_in.at[r], ens_peers[r]) for r in range(1, n)]
    area_copies = [remote(area_all.at[0], area_all.at[o], grid_peers[o]) for o in range(1, ng)]
    hid_copy = remote(hid_s.at[:, 1 - core], hidp, twin)
    lat_copy = remote(lat_hbm.at[:, 1 - core], latp, twin)
    dec_in[0] = dec_s[me]
    get_target.wait()
    tgt_s[0:s.nvars, :] = target_ref[...]
    wot[...] = wo32[...].T.astype(BF16)
    square = (s.vpad, s.vpad)
    eye = lax.broadcasted_iota(jnp.int32, square, 0) == lax.broadcasted_iota(jnp.int32, square, 1)
    column = jnp.sum(jnp.where(eye, jnp.broadcast_to(vrow_s[0:1, :], square), 0.0), axis=1, keepdims=True)
    vcol_s[...] = jnp.broadcast_to(column, vcol_s.shape)
    mine = pl.ds(pl.multiple_of(me * s.vrow, s.vrow), s.vrow)
    weight = vcol_s[mine, 0:1] * arow
    target = tgt_s[mine, :]
    for i in range(s.tiles):
        rows = pl.ds(i * s.tile, s.tile)
        v, t = pre_s[rows, :], slope_s[rows, :]
        slope_s[rows, :] = 0.5 * (1.0 + t) + 0.5 * v * (1.0 - t * t) * GELU_C * (1.0 + 3.0 * GELU_K * v * v)
    for copy in area_copies:
        copy.wait_recv()
    total = area_all[0]
    for o in range(1, ng):
        total = total + area_all[o]
    total = total[0:1, 0:1]
    scale = 1.0 / (total * float(s.nvars))
    wide = (float(ng * s.pts) * scale) * weight
    for copy in dec_copies:
        copy.wait_recv()
    members = [dec_in[r] for r in range(n)]
    slopes = [None] * n
    pairs = jnp.full((s.vrow, s.pts), float(n) * float(np.sqrt(np.float32(SMOOTH))), F32)
    for m in range(n):
        for k in range(m):
            u = members[m] - members[k]
            q = u * u + SMOOTH
            root = lax.rsqrt(q)
            pairs = pairs + 2.0 * (q * root)
            slope = u * root
            slopes[m] = slope if slopes[m] is None else slopes[m] + slope
            slopes[k] = -slope if slopes[k] is None else slopes[k] - slope
    local = pairs * (-1.0 / (2.0 * n * (n - 1.0)))
    dout_copies = []
    for r in range(n - 1, -1, -1):
        u = members[r] - target
        q = u * u + SMOOTH
        root = lax.rsqrt(q)
        local = local + (q * root) * (1.0 / n)
        d = (wide * (u * root * (1.0 / n) - slopes[r] * (1.0 / (n * (n - 1.0))))).astype(BF16)
        if r:
            dout_o[r] = d
            dout_copies.append(remote(dout_o.at[r], dout_s.at[me], ens_peers[r]))
        else:
            dout_s[me] = d
    part = jnp.sum(jnp.sum(weight * local, axis=1, keepdims=True), axis=0, keepdims=True)
    loss_e[0] = jnp.broadcast_to(part, (8, 128))
    loss_copies = [remote(loss_e.at[0], loss_e.at[r], ens_peers[r]) for r in range(1, n)]

    for copy in dout_copies:
        copy.wait_recv()
    dout_copy = remote(dout_s, doutp, twin)
    dout = dout_s[...].reshape(s.vpad, s.pts)
    dpre_copies = []
    for i in range(s.tiles):
        rows = pl.ds(i * s.tile, s.tile)
        dpre_s[rows, :] = (dot_nn(wot[rows, :], dout) * slope_s[rows, :]).astype(BF16)
        dpre_copies.append(remote(dpre_s.at[rows], dprep.at[rows], twin))

    offsets = [nz // 2] + [o for o in range(nz - 1, 0, -1) if o != nz // 2] + [0]

    def chip_at(k):
        return (chip + offsets[k]) % nz

    up, down = list(range(nb)), list(range(nb))[::-1]

    def relative(r):
        return tuple((r >> (nb - 1 - axis)) & 1 for axis in range(nb))

    def place(value, sums, send, at, r, order):
        if (r >> order[0]) & 1:
            send[at] = value.astype(BF16)
        else:
            sums[at] = value

    def start(sums, send, into, order, stage):
        index = stage_index(nb, order, stage, 1)
        if stage:
            send[index] = sums[index].astype(BF16)
        return remote(send.at[index], into, ens_peers[1 << order[stage]])

    def absorb(copy, sums, into, order, stage):
        copy.wait_recv()
        index = stage_index(nb, order, stage, 0)
        sums[index] = sums[index] + into[...].astype(F32)

    hid_copy.wait_recv()
    dout_copy.wait_recv()
    group = max(1, min(nz, 256 // s.cols))
    wide_rows = (group * s.cols, s.pts)
    doutp_all = doutp[...].reshape(s.vpad, s.pts)
    for first in range(0, nz, group):
        zs = [chip_at(k) for k in range(first, first + group)]
        own = jnp.stack([hid_s[z, core] for z in zs]).reshape(wide_rows)
        other = jnp.stack([hidp[z] for z in zs]).reshape(wide_rows)
        tmp_o[...] = (dot_nt(dout, own) + dot_nt(doutp_all, other)).reshape(n, s.vrow, group * s.cols)
        for r in range(n):
            for k in range(group):
                value = tmp_o[ens_peer(r), :, k * s.cols:(k + 1) * s.cols]
                place(value, acc_o, snd_o, relative(r) + (first + k,), r, up)
    out_copy = start(acc_o, snd_o, rcv_o[0], up, 0)

    moves = [None] * nz
    orders = (up, down)

    def first_stage(k):
        moves[k] = [start(acc.at[k, h], snd.at[k, h], rcv[0].at[k, h], orders[h], 0) for h in range(2)]

    lat_copy.wait_recv()
    for first in range(0, nz, group):
        zs = [chip_at(k) for k in range(first, first + group)]
        own = jnp.stack([lat_s[z, core] for z in zs]).reshape(wide_rows)
        other = jnp.stack([latp[z] for z in zs]).reshape(wide_rows)
        for i in range(s.tiles):
            rows = pl.ds(i * s.tile, s.tile)
            tmp[rows, :] = dot_nt(dpre_s[rows, :], own)
        for i in range(s.tiles):
            if first == 0:
                dpre_copies[i].wait_recv()
            rows = pl.ds(i * s.tile, s.tile)
            tmp[rows, :] += dot_nt(dprep[rows, :], other)
        for k in range(first, first + group):
            lanes = slice((k - first) * s.cols, (k - first + 1) * s.cols)
            for r in range(n):
                for h in range(2):
                    base = ens_peer(r) * s.rows_e + h * s.half
                    value = tmp[pl.ds(pl.multiple_of(base, s.half), s.half), lanes]
                    place(value, acc, snd, (k, h) + relative(r), r, orders[h])
            if k < AHEAD:
                first_stage(k)


    quarter = s.lat // 4

    def latent_part(j):
        at = pl.ds(j * quarter, quarter)
        glat_ref[0, at, :] = dot_tn(win_s[:, at], dpre_s[...]).astype(BF16)

    latent_part(0)
    zero = (0,) * nb
    out_moves = []

    def out_step(copy, stage):
        absorb(copy, acc_o, rcv_o[stage], up, stage)
        if stage < nb - 1:
            return start(acc_o, snd_o, rcv_o[stage + 1], up, stage + 1)
        for k in range(nz - 1):
            zsnd_o[k] = acc_o[zero + (k,)].astype(BF16)
            out_moves.append(remote(zsnd_o.at[k], zrcv_o.at[k], {"grid": chip_at(k) * 2 + core}))
        return None

    out_copy = out_step(out_copy, 0)
    latent_part(1)
    for copy in loss_copies:
        copy.wait_recv()
    here = loss_e[0]
    for r in range(1, n):
        here = here + loss_e[r]
    loss_g[0] = here
    loss_copies = [remote(loss_g.at[0], loss_g.at[o], grid_peers[o]) for o in range(1, ng)]
    ratio = float(1.0 / np.sqrt(np.float32(ng * s.pts) * np.float32(n)))
    early = len(sent)
    for step in range(nz + nb - 1):
        if step in (1, 2):
            latent_part(step + 1)
        for stage in range(nb):
            k = step - stage
            if not 0 <= k < nz:
                continue
            for h, order in enumerate(orders):
                absorb(moves[k][h], acc.at[k, h], rcv[stage].at[k, h], order, stage)
                if stage < nb - 1:
                    moves[k][h] = start(acc.at[k, h], snd.at[k, h], rcv[stage + 1].at[k, h], order, stage + 1)
            if stage == 0 and k + AHEAD < nz:
                first_stage(k + AHEAD)
            if stage == nb - 1 and k < nz - 1:
                zsnd[k] = acc[(k, slice(None)) + zero].astype(BF16)
                moves[k] = remote(zsnd.at[k], zrcv.at[k], {"grid": chip_at(k) * 2 + core})
        if step + 1 < nb:
            out_copy = out_step(out_copy, step + 1)
        if step == 2:
            for copy in sent[:early]:
                copy.wait_send()
        if step == nz + nb - 3:
            block = acc_o[zero + (nz - 1,)]
            for k in range(nz - 1):
                out_moves[k].wait_recv()
                block = block + zrcv_o[k].astype(F32)
            gall[mine, :] = ratio * block
            gathers = [remote(gall.at[mine], gall.at[mine], ens_peers[r]) for r in range(1, n)]

    block = acc[(nz - 1, slice(None)) + zero]
    for k in range(nz - 1):
        moves[k].wait_recv()
        block = block + zrcv[k].astype(F32)
    gin_ref[...] = (ratio * block).reshape(s.rows_e, s.cols)
    for copy in loss_copies:
        copy.wait_recv()
    loss = loss_g[0]
    for o in range(1, ng):
        loss = loss + loss_g[o]
    loss_ref[...] = loss[0:1, 0:1] * scale
    for copy in gathers:
        copy.wait_recv()
    gout_ref[...] = gall[0:s.nvars, :]
    for copy in sent[early:]:
        copy.wait_send()


def hand_out(*refs):
    sources, targets, held, sems = refs[:3], refs[3:6], refs[6:9], refs[9]
    reads = [pltpu.make_async_copy(x, y, sems.at[0, i]) for i, (x, y) in enumerate(zip(sources, held))]
    writes = [pltpu.make_async_copy(x, y, sems.at[1, i]) for i, (x, y) in enumerate(zip(held, targets))]
    for copy in reads:
        copy.start()
    for read, write in zip(reads, writes):
        read.wait()
        write.start()
    for copy in writes:
        copy.wait()


def per_device(n, ng, latent, w_in, w_out, target, area, var_weight):
    hid, lat = w_in.shape
    pts = latent.shape[2]
    nvars = w_out.shape[0]
    s = Sizes(n, ng, hid, lat, nvars, pts)
    nz, nb, cols = s.nz, s.nb, s.cols
    cube = (2,) * nb
    group = max(1, min(nz, 256 // cols))
    vmem = pl.BlockSpec(memory_space=pltpu.VMEM)
    hbm = pl.BlockSpec(memory_space=pltpu.HBM)
    scratch = [
        pltpu.VMEM((nz, 2, cols, pts), BF16),
        pltpu.VMEM((nz, cols, pts), BF16),
        pltpu.VMEM((hid, lat), BF16),
        pltpu.VMEM((nvars, hid), BF16),
        pltpu.VMEM((nvars, pts), F32),
        pltpu.VMEM((pts,), F32),
        pltpu.VMEM((nvars,), F32),
        pltpu.VMEM((s.vpad, hid), F32),
        pltpu.VMEM((s.vpad, hid), BF16),
        pltpu.VMEM((hid, s.vpad), BF16),
        pltpu.VMEM((nz, 2, cols, pts), BF16),
        pltpu.VMEM((nz, cols, pts), BF16),
        pltpu.VMEM((hid, pts), F32),
        pltpu.VMEM((hid, pts), F32),
        pltpu.VMEM((n, s.vrow, pts), F32),
        pltpu.VMEM((n, s.vrow, pts), F32),
        pltpu.VMEM((s.vpad, pts), F32),
        pltpu.VMEM((8, s.vpad), F32),
        pltpu.VMEM((s.vpad, 128), F32),
        pltpu.VMEM((ng, 8, 128), F32),
        pltpu.VMEM((n, s.vrow, pts), BF16),
        pltpu.VMEM((n, s.vrow, pts), BF16),
        pltpu.VMEM((n, s.vrow, pts), BF16),
        pltpu.VMEM((n, 8, 128), F32),
        pltpu.VMEM((ng, 8, 128), F32),
        pltpu.VMEM((hid, pts), BF16),
        pltpu.VMEM((hid, pts), BF16),
        pltpu.VMEM((s.vpad, cols), F32),
        pltpu.VMEM((hid, group * cols), F32),
        pltpu.VMEM((nz, 2) + cube + (s.half, cols), F32),
        pltpu.VMEM((nz, 2) + cube + (s.half, cols), BF16),
        pltpu.VMEM(cube + (nz, s.vrow, cols), F32),
        pltpu.VMEM(cube + (nz, s.vrow, cols), BF16),
        pltpu.VMEM((n, s.vrow, group * cols), F32),
        pltpu.VMEM((nz - 1, 2, s.half, cols), BF16),
        pltpu.VMEM((nz - 1, 2, s.half, cols), BF16),
        pltpu.VMEM((nz - 1, s.vrow, cols), BF16),
        pltpu.VMEM((nz - 1, s.vrow, cols), BF16),
    ]
    scratch += [pltpu.VMEM((nz, 2) + cube[1 + i:] + (s.half, cols), BF16) for i in range(nb)]
    scratch += [pltpu.VMEM(cube[1 + i:] + (nz, s.vrow, cols), BF16) for i in range(nb)]
    scratch += [
        pltpu.SemaphoreType.DMA((s.copies,)),
        pltpu.SemaphoreType.DMA((s.copies,)),
        pltpu.SemaphoreType.DMA((5 + s.tiles,)),
    ]
    loss, grad_lat, grad_in, grad_out = pl.pallas_call(
        functools.partial(kernel, s),
        out_shape=(
            jax.ShapeDtypeStruct((1, 1), F32),
            jax.ShapeDtypeStruct((1, lat, pts), BF16),
            jax.ShapeDtypeStruct((s.rows_e, cols), F32),
            jax.ShapeDtypeStruct((nvars, cols), F32),
        ),
        in_specs=[hbm] * 6,
        out_specs=(vmem,) * 4,
        scratch_shapes=scratch,
        compiler_params=pltpu.CompilerParams(
            collective_id=0, has_side_effects=True, vmem_limit_bytes=VMEM_BYTES
        ),
        name="crps_backward",
    )(latent.reshape(nz, 2, cols, pts), w_in, w_out, target, area, var_weight)
    grad_lat, grad_in, grad_out = pl.pallas_call(
        hand_out,
        out_shape=tuple(jax.ShapeDtypeStruct(x.shape, x.dtype) for x in (grad_lat, grad_in, grad_out)),
        in_specs=[hbm] * 3,
        out_specs=(hbm,) * 3,
        scratch_shapes=[pltpu.VMEM(x.shape, x.dtype) for x in (grad_lat, grad_in, grad_out)]
        + [pltpu.SemaphoreType.DMA((2, 3))],
        compiler_params=pltpu.CompilerParams(vmem_limit_bytes=VMEM_BYTES),
        name="hand_out",
    )(grad_lat, grad_in, grad_out)
    return loss[0, 0], grad_lat, grad_in, grad_out


def solution(mesh):
    in_specs = (P("ens", None, "grid"), P(), P(), P(None, "grid"), P("grid"), P())
    out_specs = (P(), P("ens", None, "grid"), P("ens", "grid"), P(None, "grid"))
    body = functools.partial(per_device, mesh.shape["ens"], mesh.shape["grid"])
    return jax.shard_map(
        body, mesh=mesh, in_specs=in_specs, out_specs=out_specs, check_vma=False
    )
```
